32 devices in a mesh: ang: 4 (over y, x), pul: 8 (over z, core).
Axes of the slice: x: 2, y: 2, z: 4, core: 2. Of those that a mesh axis runs over, the one named last changes fastest.
Arguments:
- pulses: bfloat16 [2, 1024, 16384], P(None, ('ang', 'pul')), may hold values from -6 to 6
- matched_filter: float32 [2, 16384], replicated, may hold values from -6 to 6
- interp_weights: bfloat16 [4, 8, 64, 256], P('ang', 'pul'), may hold values from -0.75 to 0.75
- offsets: int32 [4, 8, 8], P('ang', 'pul'), may hold values from 0 to 192, as said below
Outputs:
- image: float32 [32, 2, 2048], P(('ang', 'pul'))
The draws below stay inside these ranges and needn't reach their ends.
Inputs may be any that keep to these rules, and one draw needn't show every extreme that they name: `offsets`: each block's window of 64 pulses lies inside its group; the first block of every tile starts at 0 and the last at 192.
All inputs are finite; a program needn't handle non-finite values.
Results may differ from the reference program's by a relative error of at most 0.015.
Values may be sent and summed in bfloat16 or wider, within the bound.
No kernel may reach another device: no remote copies, remote signals or barrier semaphores. Data moves between devices by JAX's collectives and lax.ppermute only.
A program may use at most 64 MiB of HBM per device.

```python
import math
import jax
import jax.numpy as jnp
from jax import lax

FACTOR = 128
RANGE_BINS = 16384
BLOCK_ROWS = 32
BAND_PULSES = 64
IMAGE_COLS = 2048
GROUP_PULSES = 256
PULSES = 1024
BLOCKS = 8
IMAGE_ROWS = 32
N_ANG = 4
N_PUL = 8


def draw_offsets(key, part):
    window_span = GROUP_PULSES - BAND_PULSES
    block_index = jnp.arange(BLOCKS, dtype=jnp.int32)
    baseline = block_index * window_span // (BLOCKS - 1)
    jitter = jax.random.randint(key, (N_ANG, N_PUL, BLOCKS), -(BLOCK_ROWS // 2), BLOCK_ROWS // 2 + 1, dtype=jnp.int32)
    inside = jnp.logical_and(block_index > 0, block_index < BLOCKS - 1)
    moved = baseline + jnp.where(inside, jitter, 0)
    return jnp.clip(moved, 0, window_span).astype(jnp.int32)


def steps_of(rng, extent, pieces, least, largest):
    gain, own = 1.0, jax.random.fold_in(rng, 6)
    for axis_at, parts in pieces:
        draws = jnp.exp(jax.random.uniform(jax.random.fold_in(own, axis_at), (parts,), jnp.float32, least / len(pieces), largest / len(pieces)))
        gain = gain * jnp.repeat(draws, extent[axis_at] // parts).reshape([-1 if axis == axis_at else 1 for axis in range(len(extent))])
    return gain


def normal_values(own_key, extent, width, reach, cuts=(), held_as=jnp.bfloat16):
    level = steps_of(own_key, extent, cuts, -0.22, 0.18) if cuts else 1.0
    entries = jax.random.normal(own_key, extent, jnp.float32) * width * level
    return jnp.minimum(jnp.maximum(entries, -reach), reach).astype(held_as)


def setup_inputs(seed: int = 0) -> dict:
    splits = jax.random.split(jax.random.key(seed), 5)
    return {
        "pulses": normal_values(splits[0], (2, PULSES, RANGE_BINS), 1.0, 6.0, ((1, 32),)),
        "matched_filter": normal_values(splits[1], (2, RANGE_BINS), 1.0, 6.0, (), jnp.float32),
        "interp_weights": normal_values(splits[2], (N_ANG, N_PUL, BAND_PULSES, GROUP_PULSES), BAND_PULSES ** -0.5, 0.75, ((0, 4), (1, 8))),
        "offsets": draw_offsets(jax.random.fold_in(splits[4], 71), 0),
    }


HIGHEST_MODE = lax.Precision.HIGHEST

def range_forward(real_part, imag_part):
    row_total = real_part.shape[0]
    places = jnp.arange(FACTOR, dtype=jnp.int32)
    phase = jnp.mod(places[:, None] * places[None, :], FACTOR)
    angle = phase.astype(jnp.float32) * (-2.0 * math.pi / FACTOR)
    cos_small = lax.optimization_barrier(jnp.cos(angle).astype(jnp.bfloat16)).astype(jnp.float32)
    sin_small = lax.optimization_barrier(jnp.sin(angle).astype(jnp.bfloat16)).astype(jnp.float32)
    twist_phase = jnp.mod(places[:, None] * places[None, :], FACTOR * FACTOR)
    twist_angle = twist_phase.astype(jnp.float32) * (-2.0 * math.pi / (FACTOR * FACTOR))
    twist_cos = jnp.cos(twist_angle)
    twist_sin = jnp.sin(twist_angle)
    real_grid = real_part.astype(jnp.float32).reshape(row_total, FACTOR, FACTOR)
    imag_grid = imag_part.astype(jnp.float32).reshape(row_total, FACTOR, FACTOR)
    section_real = jnp.einsum('km,rmn->rkn', cos_small, real_grid, precision=HIGHEST_MODE) - jnp.einsum('km,rmn->rkn', sin_small, imag_grid, precision=HIGHEST_MODE)
    section_imag = jnp.einsum('km,rmn->rkn', cos_small, imag_grid, precision=HIGHEST_MODE) + jnp.einsum('km,rmn->rkn', sin_small, real_grid, precision=HIGHEST_MODE)
    turned_real = lax.optimization_barrier((section_real * twist_cos - section_imag * twist_sin).astype(jnp.bfloat16)).astype(jnp.float32)
    turned_imag = lax.optimization_barrier((section_real * twist_sin + section_imag * twist_cos).astype(jnp.bfloat16)).astype(jnp.float32)
    final_real = jnp.einsum('rkm,mj->rkj', turned_real, cos_small, precision=HIGHEST_MODE) - jnp.einsum('rkm,mj->rkj', turned_imag, sin_small, precision=HIGHEST_MODE)
    final_imag = jnp.einsum('rkm,mj->rkj', turned_real, sin_small, precision=HIGHEST_MODE) + jnp.einsum('rkm,mj->rkj', turned_imag, cos_small, precision=HIGHEST_MODE)
    length = FACTOR * FACTOR
    return (jnp.transpose(final_real, (0, 2, 1)).reshape(row_total, length), jnp.transpose(final_imag, (0, 2, 1)).reshape(row_total, length))

def resample_group(spectrum, weights, starts):
    bins_tile = RANGE_BINS // N_PUL

    def one_tile(tile_index):
        columns = lax.dynamic_slice_in_dim(spectrum, tile_index * bins_tile, bins_tile, 2)
        tile_starts = lax.dynamic_index_in_dim(starts, tile_index, 0, keepdims=False)
        tile_weights = lax.dynamic_index_in_dim(weights, tile_index, 0, keepdims=False)
        windows = jax.vmap(lambda begin_pulse: lax.dynamic_slice_in_dim(columns, begin_pulse, BAND_PULSES, 1))(tile_starts)
        kernel = tile_weights.reshape(BAND_PULSES, BLOCKS, BLOCK_ROWS).astype(jnp.float32)
        mixed = jnp.einsum('jbk,bcjn->cbkn', kernel, windows.astype(jnp.float32), precision=HIGHEST_MODE)
        return mixed.reshape(2, GROUP_PULSES, bins_tile).astype(jnp.bfloat16)
    tiles = lax.map(one_tile, jnp.arange(N_PUL, dtype=jnp.int32))
    return jnp.transpose(tiles, (1, 2, 0, 3)).reshape(2, GROUP_PULSES, RANGE_BINS)

def reference(pulses, matched_filter, interp_weights, offsets):
    image_index = jnp.arange(IMAGE_ROWS, dtype=jnp.int32)
    root_bins = math.sqrt(RANGE_BINS)

    def add_group(running, group_index):
        panel = lax.dynamic_slice_in_dim(pulses, group_index * GROUP_PULSES, GROUP_PULSES, 1)
        wave_real, wave_imag = range_forward(panel[0], panel[1])
        wave_real = wave_real / root_bins
        wave_imag = wave_imag / root_bins
        spec_real = wave_real * matched_filter[0] - wave_imag * matched_filter[1]
        spec_imag = wave_real * matched_filter[1] + wave_imag * matched_filter[0]
        spectrum = jnp.stack([spec_real, spec_imag]).astype(jnp.bfloat16)
        weights = lax.dynamic_index_in_dim(interp_weights, group_index, 0, keepdims=False)
        starts = lax.dynamic_index_in_dim(offsets, group_index, 0, keepdims=False)
        resampled = lax.optimization_barrier(resample_group(spectrum, weights, starts)).astype(jnp.float32)
        grid_rows = group_index * GROUP_PULSES + jnp.arange(GROUP_PULSES, dtype=jnp.int32)
        phase = jnp.mod((image_index[:, None] - IMAGE_ROWS // 2) * grid_rows[None, :], PULSES)
        angle = phase.astype(jnp.float32) * (2.0 * math.pi / PULSES)
        table_real = lax.optimization_barrier((jnp.cos(angle) / math.sqrt(PULSES)).astype(jnp.bfloat16)).astype(jnp.float32)
        table_imag = lax.optimization_barrier((jnp.sin(angle) / math.sqrt(PULSES)).astype(jnp.bfloat16)).astype(jnp.float32)
        part_real = jnp.dot(table_real, resampled[0], precision=HIGHEST_MODE) - jnp.dot(table_imag, resampled[1], precision=HIGHEST_MODE)
        part_imag = jnp.dot(table_real, resampled[1], precision=HIGHEST_MODE) + jnp.dot(table_imag, resampled[0], precision=HIGHEST_MODE)
        partial_value = lax.optimization_barrier(jnp.stack([part_real, part_imag], axis=1).astype(jnp.bfloat16)).astype(jnp.float32)
        return (running + partial_value, None)
    start_sum = jnp.zeros((IMAGE_ROWS, 2, RANGE_BINS), jnp.float32)
    summed, _ = lax.scan(add_group, start_sum, jnp.arange(N_ANG, dtype=jnp.int32))
    summed_wave = lax.complex(summed[:, 0], summed[:, 1])
    image_wave = jnp.fft.ifft(summed_wave, axis=-1) * math.sqrt(RANGE_BINS)
    first_column = (RANGE_BINS - IMAGE_COLS) // 2
    window = image_wave[:, first_column:first_column + IMAGE_COLS]
    return jnp.stack([jnp.real(window), jnp.imag(window)], axis=1).astype(jnp.float32)
```

```python
import functools
import math

import jax
import jax.numpy as jnp
import ml_dtypes
import numpy as np
from jax import lax
from jax.experimental import pallas as pl
from jax.experimental.pallas import tpu as pltpu
from jax.sharding import PartitionSpec as P

FACTOR = 128
BLOCK_ROWS = 32
BAND_PULSES = 64
IMAGE_COLS = 2048
CHUNK = 32

BF = jnp.bfloat16
F32 = jnp.float32


def rounded(values):
    return np.asarray(values, np.float32).astype(ml_dtypes.bfloat16)


def turns(top, bottom):
    angle = np.mod(top, bottom) * (2.0 * math.pi / bottom)
    return np.cos(angle), np.sin(angle)


def complex_matrix(cos, sin):
    return np.block([[cos, -sin], [sin, cos]])


def range_tables():
    at = np.arange(FACTOR)
    grid = at[:, None] * at[None, :]
    cos, sin = turns(-grid, FACTOR)
    table = rounded(complex_matrix(cos, sin))
    twist = np.stack(turns(-grid, FACTOR * FACTOR)).astype(np.float32)
    return table, twist


def image_tables():
    at = np.arange(FACTOR)
    grid = at[:, None] * at[None, :]
    cos, sin = turns(grid, FACTOR)
    table = rounded(complex_matrix(cos, sin))
    twist = np.stack(turns(grid, FACTOR * FACTOR)).astype(np.float32)
    count = IMAGE_COLS // FACTOR
    high = np.arange(count) + (FACTOR * FACTOR - IMAGE_COLS) // 2 // FACTOR
    cos, sin = turns(high[:, None] * at[None, :], FACTOR)
    both = complex_matrix(cos, sin).reshape(2, count, 2 * FACTOR)
    last = rounded(both.transpose(1, 0, 2).reshape(2 * count, 2 * FACTOR))
    return table, twist, last


def azimuth_tables(image_rows, group_pulses, groups):
    total = group_pulses * groups
    chunks = image_rows // CHUNK
    row = np.arange(image_rows) - image_rows // 2
    cos, sin = turns(np.arange(group_pulses)[:, None] * row[None, :], total)
    cos = rounded(cos / math.sqrt(total)).astype(np.float32).reshape(-1, chunks, CHUNK)
    sin = rounded(sin / math.sqrt(total)).astype(np.float32).reshape(-1, chunks, CHUNK)
    table = np.concatenate([cos, sin, -sin, cos, -sin, cos, -cos, -sin], axis=2)
    turn_cos, turn_sin = turns(np.arange(groups)[:, None] * group_pulses * row[None, :], total)
    turn = np.stack([turn_cos, turn_sin], axis=1).reshape(groups, 2, chunks, CHUNK)
    turn = np.where(np.abs(turn) < 1e-9, 0.0, turn)
    turn = np.tile(turn, (1, 1, 1, 4)).transpose(0, 2, 1, 3)
    return rounded(table.reshape(group_pulses, chunks * 8 * CHUNK)), turn.astype(np.float32)


HBM = pl.BlockSpec(memory_space=pltpu.HBM)
VMEM = pl.BlockSpec(memory_space=pltpu.VMEM)
UNROLL = dict(wide=16, first=4, second=4, out=16, mix=1, image=4)


def in_hbm(*arrays):
    return [pltpu.with_memory_space_constraint(jnp.asarray(a), pltpu.HBM) for a in arrays]


def fetch(pairs, sems):
    copies = [pltpu.make_async_copy(a, b, sems.at[n]) for n, (a, b) in enumerate(pairs)]
    for copy in copies:
        copy.start()
    return copies


def mixing_kernel(
    blocks, chunks, offsets_hbm, weights_hbm, table_hbm, turn_hbm, out_ref,
    offsets_ref, weights_ref, table_ref, turn_ref, first_ref, second_ref, total_ref, other_ref, sems,
):
    width = 4 * CHUNK
    chunk = pl.program_id(0)
    group = lax.axis_index("ang")
    columns = pl.ds(pl.multiple_of(chunk * 2 * width, 2 * width), 2 * width) if chunks > 1 else slice(None)
    copies = fetch(
        [
            (weights_hbm.at[0, 0], weights_ref),
            (table_hbm.at[:, columns], table_ref),
            (offsets_hbm, offsets_ref),
            (turn_hbm.at[group, chunk], turn_ref),
        ],
        sems,
    )
    total_ref[...] = jnp.zeros_like(total_ref)
    other_ref[...] = jnp.zeros_like(other_ref)
    copies[0].wait()
    copies[1].wait()
    weights = weights_ref[...]
    column = lax.broadcasted_iota(jnp.int32, weights.shape, 1) // BLOCK_ROWS

    def multiply(block, carry):
        own = jnp.where(column == block, weights.astype(F32), 0.0).astype(BF)
        product = jnp.dot(own, table_ref[...], preferred_element_type=F32)
        first_ref[block] = product[:, :width]
        second_ref[block] = product[:, width:]
        return carry

    lax.fori_loop(0, blocks, multiply, 0, unroll=blocks <= 8)
    copies[2].wait()
    copies[3].wait()

    def place(block, carry):
        window = pl.ds(offsets_ref[0, 0, block], BAND_PULSES)
        total_ref[window, :] += first_ref[block]
        other_ref[window, :] += second_ref[block]
        return carry

    lax.fori_loop(0, blocks, place, 0)
    turn = turn_ref[...]
    out_ref[...] = (total_ref[...] * turn[0:1] + other_ref[...] * turn[1:2]).astype(BF)


def mixing(offsets, weights, table, turn):
    group_pulses, width = weights.shape[3], 4 * CHUNK
    chunks, blocks = table.shape[1] // (2 * width), offsets.shape[2]
    return pl.pallas_call(
        functools.partial(mixing_kernel, blocks, chunks),
        grid=(chunks,),
        out_shape=jax.ShapeDtypeStruct((group_pulses, chunks * width), BF),
        in_specs=[HBM] * 4,
        out_specs=pl.BlockSpec((group_pulses, width), lambda c: (0, c)),
        scratch_shapes=[
            pltpu.SMEM(offsets.shape, jnp.int32),
            pltpu.VMEM(weights.shape[2:], BF),
            pltpu.VMEM((group_pulses, 2 * width), BF),
            pltpu.VMEM(turn.shape[2:], F32),
            pltpu.VMEM((blocks, BAND_PULSES, width), F32),
            pltpu.VMEM((blocks, BAND_PULSES, width), F32),
            pltpu.VMEM((group_pulses, width), F32),
            pltpu.VMEM((group_pulses, width), F32),
            pltpu.SemaphoreType.DMA((4,)),
        ],
        compiler_params=pltpu.CompilerParams(vmem_limit_bytes=24 * 2**20),
        name="mixing",
    )(*in_hbm(offsets, weights, table, turn))


def turn_by(wave, j, twist_ref):
    real = wave[:FACTOR, j * FACTOR : (j + 1) * FACTOR]
    imag = wave[FACTOR:, j * FACTOR : (j + 1) * FACTOR]
    cos, sin = twist_ref[0], twist_ref[1]
    return jnp.concatenate([(real * cos - imag * sin).astype(BF), (real * sin + imag * cos).astype(BF)], axis=1)


def times_transposed(left, right):
    return lax.dot_general(left, right, (((1,), (1,)), ((), ())), preferred_element_type=F32)


def range_kernel(
    rows, pulses_hbm, filter_hbm, table_hbm, twist_hbm, out_ref,
    pulses_ref, filter_ref, table_ref, twist_ref, wide_ref, turned_ref, spec_ref, sems,
):
    parts = 8
    length = FACTOR // parts
    pieces = [
        (pulses_hbm.at[:, :, pl.ds(h * length * FACTOR, length * FACTOR)], pulses_ref.at[h]) for h in range(parts)
    ]
    copies = fetch(
        pieces + [(table_hbm, table_ref), (twist_hbm, twist_ref), (filter_hbm, filter_ref)], sems
    )
    for h in range(parts):
        copies[h].wait()
        for m in range(length):
            for c in range(2):
                wide_ref[c, (h * length + m) * rows : (h * length + m + 1) * rows, :] = pulses_ref[
                    h, c, :, m * FACTOR : (m + 1) * FACTOR
                ].astype(F32)
    copies[parts].wait()
    copies[parts + 1].wait()
    pair = 2

    def first(s, carry):
        sides = [
            jnp.concatenate(
                [wide_ref[c, pl.ds(s * pair + j, FACTOR, stride=rows), :].astype(BF) for c in range(2)], axis=0
            )
            for j in range(pair)
        ]
        section = jnp.dot(table_ref[...], jnp.concatenate(sides, axis=1), preferred_element_type=F32)
        for j in range(pair):
            turned_ref[s, j * FACTOR : (j + 1) * FACTOR, :] = turn_by(section, j, twist_ref)
        return carry

    lax.fori_loop(0, rows // pair, first, 0, unroll=UNROLL["first"])
    copies[parts + 2].wait()
    filter_real = filter_ref[:, 0, :] * (1.0 / FACTOR)
    filter_imag = filter_ref[:, 1, :] * (1.0 / FACTOR)
    spec_view = spec_ref

    def second(s, carry):
        wave = times_transposed(table_ref[...], turned_ref[s])
        for j in range(pair):
            p = s * pair + j
            real = wave[:FACTOR, j * FACTOR : (j + 1) * FACTOR]
            imag = wave[FACTOR:, j * FACTOR : (j + 1) * FACTOR]
            spec_view[pl.ds(p, FACTOR, stride=2 * rows), :] = real * filter_real - imag * filter_imag
            spec_view[pl.ds(rows + p, FACTOR, stride=2 * rows), :] = real * filter_imag + imag * filter_real
        return carry

    lax.fori_loop(0, rows // pair, second, 0, unroll=UNROLL["second"])

    def narrow(k2, carry):
        begin = pl.multiple_of(k2 * 2 * rows, 2 * rows)
        out_ref[k2] = spec_ref[pl.ds(begin, 2 * rows), :].astype(BF)
        return carry

    lax.fori_loop(0, FACTOR, narrow, 0, unroll=UNROLL["out"])


def range_forward(pulses, matched_filter, table, twist):
    rows, parts = pulses.shape[1], 8
    filters = matched_filter.reshape(2, FACTOR, FACTOR).transpose(1, 0, 2)
    return pl.pallas_call(
        functools.partial(range_kernel, rows),
        out_shape=jax.ShapeDtypeStruct((FACTOR, 2 * rows, FACTOR), BF),
        in_specs=[HBM] * 4,
        out_specs=VMEM,
        scratch_shapes=[
            pltpu.VMEM((parts, 2, rows, FACTOR * FACTOR // parts), BF),
            pltpu.VMEM((FACTOR, 2, FACTOR), F32),
            pltpu.VMEM((2 * FACTOR, 2 * FACTOR), BF),
            pltpu.VMEM((2, FACTOR, FACTOR), F32),
            pltpu.VMEM((2, FACTOR * rows, FACTOR), F32),
            pltpu.VMEM((rows // 2, 2 * FACTOR, 2 * FACTOR), BF),
            pltpu.VMEM((FACTOR * 2 * rows, FACTOR), F32),
            pltpu.SemaphoreType.DMA((parts + 3,)),
        ],
        compiler_params=pltpu.CompilerParams(vmem_limit_bytes=32 * 2**20),
        cost_estimate=pl.CostEstimate(flops=10**10, bytes_accessed=2**22, transcendentals=0),
        name="range_forward",
    )(*in_hbm(pulses, filters, table, twist))


def image_kernel(rows, tiles, spec_ref, mix_ref, table_ref, twist_ref, last_ref, out_ref, mixed_ref):
    wide = 2 * CHUNK
    for t in range(tiles):
        mix = mix_ref[t].astype(F32)
        mix = jnp.concatenate([mix[:, :wide], mix[:, wide:]], axis=0).T.astype(BF)
        for k2 in range(t * (FACTOR // tiles), (t + 1) * (FACTOR // tiles)):
            mixed_ref[k2 * wide : (k2 + 1) * wide, :] = jnp.dot(mix, spec_ref[k2], preferred_element_type=F32)
    pair = 2

    def step(s, carry):
        sides = [
            jnp.concatenate(
                [
                    mixed_ref[pl.ds(c * CHUNK + s * pair + j, FACTOR, stride=wide), :].astype(BF)
                    for c in range(2)
                ],
                axis=0,
            )
            for j in range(pair)
        ]
        wave = jnp.dot(table_ref[...], jnp.concatenate(sides, axis=1), preferred_element_type=F32)
        turned = jnp.concatenate([turn_by(wave, j, twist_ref) for j in range(pair)], axis=0)
        window = times_transposed(last_ref[...], turned) * (1.0 / FACTOR)
        for j in range(pair):
            out_ref[s * pair + j] = window[:, j * FACTOR : (j + 1) * FACTOR].astype(BF)
        return carry

    lax.fori_loop(0, CHUNK // pair, step, 0, unroll=UNROLL["image"])


def image_part(spec, mix, table, twist, last):
    tiles, rows = mix.shape[0], mix.shape[1]
    chunks = mix.shape[2] // (4 * CHUNK)
    whole = lambda array: pl.BlockSpec(array.shape, lambda c: (0,) * array.ndim)
    high = last.shape[0]
    return pl.pallas_call(
        functools.partial(image_kernel, rows, tiles),
        grid=(chunks,),
        out_shape=jax.ShapeDtypeStruct((chunks * CHUNK, high, FACTOR), BF),
        in_specs=[
            whole(spec),
            pl.BlockSpec((tiles, rows, 4 * CHUNK), lambda c: (0, 0, c)),
            whole(table),
            whole(twist),
            whole(last),
        ],
        out_specs=pl.BlockSpec((CHUNK, high, FACTOR), lambda c: (c, 0, 0)),
        scratch_shapes=[pltpu.VMEM((FACTOR * 2 * CHUNK, FACTOR), F32)],
        compiler_params=pltpu.CompilerParams(vmem_limit_bytes=32 * 2**20),
        name="image_part",
    )(spec, mix, table, twist, last)


def local(pulses, matched_filter, interp_weights, offsets):
    pul_count, ang_count = lax.axis_size("pul"), lax.axis_size("ang")
    image_rows, rows = pul_count * ang_count, pulses.shape[1]
    azimuth, turn = azimuth_tables(image_rows, rows * pul_count, ang_count)
    mix = mixing(offsets, interp_weights, azimuth, turn)
    mix = lax.all_to_all(
        mix.reshape(pul_count, rows, mix.shape[1]), "pul", split_axis=0, concat_axis=0, tiled=True
    )
    spec = range_forward(pulses, matched_filter, *range_tables())
    part = image_part(spec, mix, *image_tables())
    parts = lax.all_to_all(part, ("ang", "pul"), split_axis=0, concat_axis=0, tiled=True)
    image = jnp.sum(parts.astype(F32), axis=0)
    return image.reshape(-1, 2, FACTOR).transpose(1, 0, 2).reshape(1, 2, IMAGE_COLS)


def solution(mesh):
    placed = (
        P(None, ("ang", "pul"), None),
        P(),
        P("ang", "pul", None, None),
        P("ang", "pul", None),
    )
    return jax.shard_map(
        local, mesh=mesh, in_specs=placed, out_specs=P(("ang", "pul"), None, None), check_vma=False
    )
```

```python
import functools
import math

import jax
import jax.numpy as jnp
import ml_dtypes
import numpy as np
from jax import lax
from jax.experimental import pallas as pl
from jax.experimental.pallas import tpu as pltpu
from jax.sharding import PartitionSpec as P

FACTOR = 128
BLOCK_ROWS = 32
BAND_PULSES = 64
IMAGE_COLS = 2048
CHUNK = 32

BF = jnp.bfloat16
F32 = jnp.float32


def rounded(values):
    return np.asarray(values, np.float32).astype(ml_dtypes.bfloat16)


def turns(top, bottom):
    angle = np.mod(top, bottom) * (2.0 * math.pi / bottom)
    return np.cos(angle), np.sin(angle)


def complex_matrix(cos, sin):
    return np.block([[cos, -sin], [sin, cos]])


def range_tables():
    at = np.arange(FACTOR)
    grid = at[:, None] * at[None, :]
    cos, sin = turns(-grid, FACTOR)
    table = rounded(complex_matrix(cos, sin))
    twist = np.stack(turns(-grid, FACTOR * FACTOR)).astype(np.float32)
    return table, twist


def image_tables():
    at = np.arange(FACTOR)
    grid = at[:, None] * at[None, :]
    cos, sin = turns(grid, FACTOR)
    table = rounded(complex_matrix(cos, sin))
    twist = np.stack(turns(grid, FACTOR * FACTOR)).astype(np.float32)
    count = IMAGE_COLS // FACTOR
    high = np.arange(count) + (FACTOR * FACTOR - IMAGE_COLS) // 2 // FACTOR
    cos, sin = turns(high[:, None] * at[None, :], FACTOR)
    both = complex_matrix(cos, sin).reshape(2, count, 2 * FACTOR)
    last = rounded(both.transpose(1, 0, 2).reshape(2 * count, 2 * FACTOR))
    return table, twist, last


def azimuth_tables(image_rows, group_pulses, groups):
    total = group_pulses * groups
    chunks = image_rows // CHUNK
    row = np.arange(image_rows) - image_rows // 2
    cos, sin = turns(np.arange(group_pulses)[:, None] * row[None, :], total)
    cos = rounded(cos / math.sqrt(total)).astype(np.float32).reshape(-1, chunks, CHUNK)
    sin = rounded(sin / math.sqrt(total)).astype(np.float32).reshape(-1, chunks, CHUNK)
    table = np.concatenate([cos, sin, -sin, cos, -sin, cos, -cos, -sin], axis=2)
    turn_cos, turn_sin = turns(np.arange(groups)[:, None] * group_pulses * row[None, :], total)
    turn = np.stack([turn_cos, turn_sin], axis=1).reshape(groups, 2, chunks, CHUNK)
    turn = np.where(np.abs(turn) < 1e-9, 0.0, turn)
    turn = np.tile(turn, (1, 1, 1, 4)).transpose(0, 2, 1, 3)
    return rounded(table.reshape(group_pulses, chunks * 8 * CHUNK)), turn.astype(np.float32)


HBM = pl.BlockSpec(memory_space=pltpu.HBM)
VMEM = pl.BlockSpec(memory_space=pltpu.VMEM)
PAD = 1
UNROLL = dict(first=8, second=8, out=2, image=8)


def in_hbm(*arrays):
    return [pltpu.with_memory_space_constraint(jnp.asarray(a), pltpu.HBM) for a in arrays]


def fetch(pairs, sems):
    copies = [pltpu.make_async_copy(a, b, sems.at[n]) for n, (a, b) in enumerate(pairs)]
    for copy in copies:
        copy.start()
    return copies


def mixing_kernel(
    blocks, chunks, offsets_hbm, weights_hbm, table_hbm, turn_hbm, out_ref,
    offsets_ref, weights_ref, table_ref, turn_ref, first_ref, second_ref, total_ref, other_ref, sems,
):
    width = 4 * CHUNK
    chunk = pl.program_id(0)
    group = lax.axis_index("ang")
    columns = pl.ds(pl.multiple_of(chunk * 2 * width, 2 * width), 2 * width) if chunks > 1 else slice(None)
    copies = fetch(
        [
            (weights_hbm.at[0, 0], weights_ref),
            (table_hbm.at[:, columns], table_ref),
            (offsets_hbm, offsets_ref),
            (turn_hbm.at[group, chunk], turn_ref),
        ],
        sems,
    )
    total_ref[...] = jnp.zeros_like(total_ref)
    other_ref[...] = jnp.zeros_like(other_ref)
    copies[0].wait()
    copies[1].wait()
    weights = weights_ref[...]
    column = lax.broadcasted_iota(jnp.int32, weights.shape, 1) // BLOCK_ROWS

    def multiply(block, carry):
        own = jnp.where(column == block, weights.astype(F32), 0.0).astype(BF)
        product = jnp.dot(own, table_ref[...], preferred_element_type=F32)
        first_ref[block] = product[:, :width]
        second_ref[block] = product[:, width:]
        return carry

    lax.fori_loop(0, blocks, multiply, 0, unroll=blocks <= 8)
    copies[2].wait()
    copies[3].wait()

    def place(block, carry):
        window = pl.ds(offsets_ref[0, 0, block], BAND_PULSES)
        total_ref[window, :] += first_ref[block]
        other_ref[window, :] += second_ref[block]
        return carry

    lax.fori_loop(0, blocks, place, 0)
    turn = turn_ref[...]
    out_ref[...] = (total_ref[...] * turn[0:1] + other_ref[...] * turn[1:2]).astype(BF)


def mixing(offsets, weights, table, turn):
    group_pulses, width = weights.shape[3], 4 * CHUNK
    chunks, blocks = table.shape[1] // (2 * width), offsets.shape[2]
    return pl.pallas_call(
        functools.partial(mixing_kernel, blocks, chunks),
        grid=(chunks,),
        out_shape=jax.ShapeDtypeStruct((group_pulses, chunks * width), BF),
        in_specs=[HBM] * 4,
        out_specs=pl.BlockSpec((group_pulses, width), lambda c: (0, c)),
        scratch_shapes=[
            pltpu.SMEM(offsets.shape, jnp.int32),
            pltpu.VMEM(weights.shape[2:], BF),
            pltpu.VMEM((group_pulses, 2 * width), BF),
            pltpu.VMEM(turn.shape[2:], F32),
            pltpu.VMEM((blocks, BAND_PULSES, width), F32),
            pltpu.VMEM((blocks, BAND_PULSES, width), F32),
            pltpu.VMEM((group_pulses, width), F32),
            pltpu.VMEM((group_pulses, width), F32),
            pltpu.SemaphoreType.DMA((4,)),
        ],
        compiler_params=pltpu.CompilerParams(vmem_limit_bytes=24 * 2**20),
        name="mixing",
    )(*in_hbm(offsets, weights, table, turn))


def turn_by(wave, j, twist_ref):
    real = wave[:FACTOR, j * FACTOR : (j + 1) * FACTOR]
    imag = wave[FACTOR:, j * FACTOR : (j + 1) * FACTOR]
    cos, sin = twist_ref[0], twist_ref[1]
    return jnp.concatenate([(real * cos - imag * sin).astype(BF), (real * sin + imag * cos).astype(BF)], axis=1)


def times_transposed(left, right):
    return lax.dot_general(left, right, (((1,), (1,)), ((), ())), preferred_element_type=F32)


def range_kernel(
    rows, pulses_hbm, filter_hbm, table_hbm, twist_hbm, out_ref,
    pulses_ref, filter_ref, table_ref, twist_ref, wide_ref, turned_ref, spec_ref, sems,
):
    parts = 8
    length = FACTOR // parts
    pieces = [
        (pulses_hbm.at[:, :, pl.ds(h * length * FACTOR, length * FACTOR)], pulses_ref.at[h]) for h in range(parts)
    ]
    copies = fetch(
        pieces + [(table_hbm, table_ref), (twist_hbm, twist_ref), (filter_hbm, filter_ref)], sems
    )
    for h in range(parts):
        copies[h].wait()
        for m in range(length):
            for c in range(2):
                wide_ref[c, pl.ds((h * length + m) * (rows + PAD), rows), :] = pulses_ref[
                    h, c, :, m * FACTOR : (m + 1) * FACTOR
                ].astype(F32)
    copies[parts].wait()
    copies[parts + 1].wait()
    pair = 2

    def first(s, carry):
        sides = [
            jnp.concatenate(
                [wide_ref[c, pl.ds(s * pair + j, FACTOR, stride=rows + PAD), :].astype(BF) for c in range(2)], axis=0
            )
            for j in range(pair)
        ]
        section = jnp.dot(table_ref[...], jnp.concatenate(sides, axis=1), preferred_element_type=F32)
        for j in range(pair):
            turned_ref[s, j * FACTOR : (j + 1) * FACTOR, :] = turn_by(section, j, twist_ref)
        return carry

    lax.fori_loop(0, rows // pair, first, 0, unroll=UNROLL["first"])
    copies[parts + 2].wait()
    filter_real = filter_ref[:, 0, :] * (1.0 / FACTOR)
    filter_imag = filter_ref[:, 1, :] * (1.0 / FACTOR)
    spec_view = spec_ref

    def second(s, carry):
        wave = times_transposed(table_ref[...], turned_ref[s])
        for j in range(pair):
            p = s * pair + j
            real = wave[:FACTOR, j * FACTOR : (j + 1) * FACTOR]
            imag = wave[FACTOR:, j * FACTOR : (j + 1) * FACTOR]
            spec_view[pl.ds(p, FACTOR, stride=2 * rows + PAD), :] = real * filter_real - imag * filter_imag
            spec_view[pl.ds(rows + p, FACTOR, stride=2 * rows + PAD), :] = real * filter_imag + imag * filter_real
        return carry

    lax.fori_loop(0, rows // pair, second, 0, unroll=UNROLL["second"])

    def narrow(step, carry):
        begin = pl.multiple_of(step * 8 * (2 * rows + PAD), 8)
        for n in range(8):
            out_ref[step * 8 + n] = spec_ref[pl.ds(begin + n * (2 * rows + PAD), 2 * rows), :].astype(BF)
        return carry

    lax.fori_loop(0, FACTOR // 8, narrow, 0, unroll=UNROLL["out"])


def range_forward(pulses, matched_filter, table, twist):
    rows, parts = pulses.shape[1], 8
    filters = matched_filter.reshape(2, FACTOR, FACTOR).transpose(1, 0, 2)
    return pl.pallas_call(
        functools.partial(range_kernel, rows),
        out_shape=jax.ShapeDtypeStruct((FACTOR, 2 * rows, FACTOR), BF),
        in_specs=[HBM] * 4,
        out_specs=VMEM,
        scratch_shapes=[
            pltpu.VMEM((parts, 2, rows, FACTOR * FACTOR // parts), BF),
            pltpu.VMEM((FACTOR, 2, FACTOR), F32),
            pltpu.VMEM((2 * FACTOR, 2 * FACTOR), BF),
            pltpu.VMEM((2, FACTOR, FACTOR), F32),
            pltpu.VMEM((2, FACTOR * (rows + PAD), FACTOR), F32),
            pltpu.VMEM((rows // 2, 2 * FACTOR, 2 * FACTOR), BF),
            pltpu.VMEM((FACTOR * (2 * rows + PAD), FACTOR), F32),
            pltpu.SemaphoreType.DMA((parts + 3,)),
        ],
        compiler_params=pltpu.CompilerParams(vmem_limit_bytes=32 * 2**20),
        cost_estimate=pl.CostEstimate(flops=10**10, bytes_accessed=2**22, transcendentals=0),
        name="range_forward",
    )(*in_hbm(pulses, filters, table, twist))


def image_kernel(rows, tiles, spec_ref, mix_ref, table_ref, twist_ref, last_ref, out_ref, mixed_ref):
    wide = 2 * CHUNK
    for t in range(tiles):
        mix = mix_ref[t].astype(F32)
        mix = jnp.concatenate([mix[:, :wide], mix[:, wide:]], axis=0).T.astype(BF)
        for k2 in range(t * (FACTOR // tiles), (t + 1) * (FACTOR // tiles)):
            mixed_ref[pl.ds(k2 * (wide + PAD), wide), :] = jnp.dot(mix, spec_ref[k2], preferred_element_type=F32)
    pair = 2

    def step(s, carry):
        sides = [
            jnp.concatenate(
                [
                    mixed_ref[pl.ds(c * CHUNK + s * pair + j, FACTOR, stride=wide + PAD), :].astype(BF)
                    for c in range(2)
                ],
                axis=0,
            )
            for j in range(pair)
        ]
        wave = jnp.dot(table_ref[...], jnp.concatenate(sides, axis=1), preferred_element_type=F32)
        turned = jnp.concatenate([turn_by(wave, j, twist_ref) for j in range(pair)], axis=0)
        window = times_transposed(last_ref[...], turned) * (1.0 / FACTOR)
        for j in range(pair):
            out_ref[s * pair + j] = window[:, j * FACTOR : (j + 1) * FACTOR].astype(BF)
        return carry

    lax.fori_loop(0, CHUNK // pair, step, 0, unroll=UNROLL["image"])


def image_part(spec, mix, table, twist, last):
    tiles, rows = mix.shape[0], mix.shape[1]
    chunks = mix.shape[2] // (4 * CHUNK)
    whole = lambda array: pl.BlockSpec(array.shape, lambda c: (0,) * array.ndim)
    high = last.shape[0]
    return pl.pallas_call(
        functools.partial(image_kernel, rows, tiles),
        grid=(chunks,),
        out_shape=jax.ShapeDtypeStruct((chunks * CHUNK, high, FACTOR), BF),
        in_specs=[
            whole(spec),
            pl.BlockSpec((tiles, rows, 4 * CHUNK), lambda c: (0, 0, c)),
            whole(table),
            whole(twist),
            whole(last),
        ],
        out_specs=pl.BlockSpec((CHUNK, high, FACTOR), lambda c: (c, 0, 0)),
        scratch_shapes=[pltpu.VMEM((FACTOR * (2 * CHUNK + PAD), FACTOR), F32)],
        compiler_params=pltpu.CompilerParams(vmem_limit_bytes=32 * 2**20),
        name="image_part",
    )(spec, mix, table, twist, last)


def local(pulses, matched_filter, interp_weights, offsets):
    pul_count, ang_count = lax.axis_size("pul"), lax.axis_size("ang")
    image_rows, rows = pul_count * ang_count, pulses.shape[1]
    azimuth, turn = azimuth_tables(image_rows, rows * pul_count, ang_count)
    mix = mixing(offsets, interp_weights, azimuth, turn)
    mix = lax.all_to_all(
        mix.reshape(pul_count, rows, mix.shape[1]), "pul", split_axis=0, concat_axis=0, tiled=True
    )
    spec = range_forward(pulses, matched_filter, *range_tables())
    part = image_part(spec, mix, *image_tables())
    parts = lax.all_to_all(part, ("ang", "pul"), split_axis=0, concat_axis=0, tiled=True)
    image = jnp.sum(parts.astype(F32), axis=0)
    return image.reshape(-1, 2, FACTOR).transpose(1, 0, 2).reshape(1, 2, IMAGE_COLS)


def solution(mesh):
    placed = (
        P(None, ("ang", "pul"), None),
        P(),
        P("ang", "pul", None, None),
        P("ang", "pul", None),
    )
    return jax.shard_map(
        local, mesh=mesh, in_specs=placed, out_specs=P(("ang", "pul"), None, None), check_vma=False
    )
```

```python
import functools
import math

import jax
import jax.numpy as jnp
import ml_dtypes
import numpy as np
from jax import lax
from jax.experimental import pallas as pl
from jax.experimental.pallas import tpu as pltpu
from jax.sharding import PartitionSpec as P

FACTOR = 128
BLOCK_ROWS = 32
BAND_PULSES = 64
IMAGE_COLS = 2048
CHUNK = 32

BF = jnp.bfloat16
F32 = jnp.float32


def rounded(values):
    return np.asarray(values, np.float32).astype(ml_dtypes.bfloat16)


def turns(top, bottom):
    angle = np.mod(top, bottom) * (2.0 * math.pi / bottom)
    return np.cos(angle), np.sin(angle)


def complex_matrix(cos, sin):
    return np.block([[cos, -sin], [sin, cos]])


def range_tables():
    at = np.arange(FACTOR)
    grid = at[:, None] * at[None, :]
    cos, sin = turns(-grid, FACTOR)
    table = rounded(complex_matrix(cos, sin))
    twist = np.stack(turns(-grid, FACTOR * FACTOR)).astype(np.float32)
    return table, twist


def image_tables():
    at = np.arange(FACTOR)
    grid = at[:, None] * at[None, :]
    cos, sin = turns(grid, FACTOR)
    table = rounded(complex_matrix(cos, sin))
    twist = np.stack(turns(grid, FACTOR * FACTOR)).astype(np.float32)
    count = IMAGE_COLS // FACTOR
    high = np.arange(count) + (FACTOR * FACTOR - IMAGE_COLS) // 2 // FACTOR
    cos, sin = turns(high[:, None] * at[None, :], FACTOR)
    both = complex_matrix(cos, sin).reshape(2, count, 2 * FACTOR)
    last = rounded(both.transpose(1, 0, 2).reshape(2 * count, 2 * FACTOR))
    return table, twist, last


def azimuth_tables(image_rows, group_pulses, groups):
    total = group_pulses * groups
    chunks = image_rows // CHUNK
    row = np.arange(image_rows) - image_rows // 2
    cos, sin = turns(np.arange(group_pulses)[:, None] * row[None, :], total)
    cos = rounded(cos / math.sqrt(total)).astype(np.float32).reshape(-1, chunks, CHUNK)
    sin = rounded(sin / math.sqrt(total)).astype(np.float32).reshape(-1, chunks, CHUNK)
    table = np.concatenate([cos, sin, -sin, cos], axis=2)
    turn_cos, turn_sin = turns(np.arange(groups)[:, None] * group_pulses * row[None, :], total)
    turn = np.stack([turn_cos, turn_sin], axis=1).reshape(groups, 2, chunks, CHUNK)
    turn = np.where(np.abs(turn) < 1e-9, 0.0, turn)
    turn = np.tile(turn, (1, 1, 1, 4))
    turn[:, 1, :, 2 * CHUNK :] *= -1.0
    turn = turn.transpose(0, 2, 1, 3)
    return rounded(table.reshape(group_pulses, chunks * 4 * CHUNK)), turn.astype(np.float32)


HBM = pl.BlockSpec(memory_space=pltpu.HBM)
VMEM = pl.BlockSpec(memory_space=pltpu.VMEM)
PAD = 1
UNROLL = dict(first=8, second=8, out=2, image=16)


def in_hbm(*arrays):
    return [pltpu.with_memory_space_constraint(jnp.asarray(a), pltpu.HBM) for a in arrays]


def fetch(pairs, sems):
    copies = [pltpu.make_async_copy(a, b, sems.at[n]) for n, (a, b) in enumerate(pairs)]
    for copy in copies:
        copy.start()
    return copies


def mixing_kernel(
    blocks, chunks, offsets_hbm, weights_hbm, table_hbm, turn_hbm, out_ref,
    offsets_ref, weights_ref, table_ref, turn_ref, product_ref, total_ref, sems,
):
    width = 4 * CHUNK
    copies = fetch(
        [
            (weights_hbm.at[0, 0], weights_ref),
            (table_hbm, table_ref),
            (offsets_hbm, offsets_ref),
            (turn_hbm.at[lax.axis_index("ang")], turn_ref),
        ],
        sems,
    )
    for copy in copies:
        copy.wait()
    weights = weights_ref[...]
    column = lax.broadcasted_iota(jnp.int32, weights.shape, 1) // BLOCK_ROWS

    def make(chunk):
        columns = pl.ds(pl.multiple_of(chunk * width, width), width)
        total_ref[...] = jnp.zeros_like(total_ref)
        table = table_ref[:, columns]

        def multiply(block, carry):
            own = jnp.where(column == block, weights.astype(F32), 0.0).astype(BF)
            product_ref[block] = jnp.dot(own, table, preferred_element_type=F32)
            return carry

        lax.fori_loop(0, blocks, multiply, 0, unroll=blocks <= 8)

        def place(block, carry):
            window = pl.ds(offsets_ref[0, 0, block], BAND_PULSES)
            total_ref[window, :] += product_ref[block]
            return carry

        lax.fori_loop(0, blocks, place, 0)
        turn = turn_ref[chunk]
        total = total_ref[...]
        other = pltpu.roll(total, width // 2, 1)
        out_ref[:, columns] = (total * turn[0:1] + other * turn[1:2]).astype(BF)

    if chunks == 1:
        make(0)
    else:
        pl.loop(0, chunks)(make)


def mixing(offsets, weights, table, turn):
    group_pulses, width = weights.shape[3], 4 * CHUNK
    chunks, blocks = table.shape[1] // width, offsets.shape[2]
    return pl.pallas_call(
        functools.partial(mixing_kernel, blocks, chunks),
        out_shape=jax.ShapeDtypeStruct((group_pulses, chunks * width), BF),
        in_specs=[HBM] * 4,
        out_specs=VMEM,
        scratch_shapes=[
            pltpu.SMEM(offsets.shape, jnp.int32),
            pltpu.VMEM(weights.shape[2:], BF),
            pltpu.VMEM(table.shape, BF),
            pltpu.VMEM(turn.shape[1:], F32),
            pltpu.VMEM((blocks, BAND_PULSES, width), F32),
            pltpu.VMEM((group_pulses, width), F32),
            pltpu.SemaphoreType.DMA((4,)),
        ],
        compiler_params=pltpu.CompilerParams(vmem_limit_bytes=24 * 2**20),
        name="mixing",
    )(*in_hbm(offsets, weights, table, turn))


def turn_by(wave, j, twist_ref):
    real = wave[:FACTOR, j * FACTOR : (j + 1) * FACTOR]
    imag = wave[FACTOR:, j * FACTOR : (j + 1) * FACTOR]
    cos, sin = twist_ref[0], twist_ref[1]
    return jnp.concatenate([(real * cos - imag * sin).astype(BF), (real * sin + imag * cos).astype(BF)], axis=1)


def times_transposed(left, right):
    return lax.dot_general(left, right, (((1,), (1,)), ((), ())), preferred_element_type=F32)


def range_kernel(
    rows, pulses_hbm, filter_hbm, table_hbm, twist_hbm, out_ref,
    pulses_ref, filter_ref, table_ref, twist_ref, wide_ref, turned_ref, spec_ref, sems,
):
    parts = 8
    length = FACTOR // parts
    pieces = [
        (pulses_hbm.at[:, :, pl.ds(h * length * FACTOR, length * FACTOR)], pulses_ref.at[h]) for h in range(parts)
    ]
    copies = fetch(
        pieces + [(table_hbm, table_ref), (twist_hbm, twist_ref), (filter_hbm, filter_ref)], sems
    )
    for h in range(parts):
        copies[h].wait()
        for m in range(length):
            for c in range(2):
                wide_ref[c, pl.ds((h * length + m) * (rows + PAD), rows), :] = pulses_ref[
                    h, c, :, m * FACTOR : (m + 1) * FACTOR
                ].astype(F32)
    copies[parts].wait()
    copies[parts + 1].wait()
    pair = 2

    def first(s, carry):
        sides = [
            jnp.concatenate(
                [wide_ref[c, pl.ds(s * pair + j, FACTOR, stride=rows + PAD), :].astype(BF) for c in range(2)], axis=0
            )
            for j in range(pair)
        ]
        section = jnp.dot(table_ref[...], jnp.concatenate(sides, axis=1), preferred_element_type=F32)
        for j in range(pair):
            turned_ref[s, j * FACTOR : (j + 1) * FACTOR, :] = turn_by(section, j, twist_ref)
        return carry

    lax.fori_loop(0, rows // pair, first, 0, unroll=UNROLL["first"])
    copies[parts + 2].wait()
    filter_real = filter_ref[:, 0, :] * (1.0 / FACTOR)
    filter_imag = filter_ref[:, 1, :] * (1.0 / FACTOR)

    def second(s, carry):
        wave = times_transposed(table_ref[...], turned_ref[s])
        for j in range(pair):
            p = s * pair + j
            real = wave[:FACTOR, j * FACTOR : (j + 1) * FACTOR]
            imag = wave[FACTOR:, j * FACTOR : (j + 1) * FACTOR]
            spec_ref[pl.ds(p, FACTOR, stride=2 * rows + PAD), :] = real * filter_real - imag * filter_imag
            spec_ref[pl.ds(rows + p, FACTOR, stride=2 * rows + PAD), :] = real * filter_imag + imag * filter_real
        return carry

    lax.fori_loop(0, rows // pair, second, 0, unroll=UNROLL["second"])

    def narrow(step, carry):
        begin = pl.multiple_of(step * 8 * (2 * rows + PAD), 8)
        for n in range(8):
            out_ref[step * 8 + n] = spec_ref[pl.ds(begin + n * (2 * rows + PAD), 2 * rows), :].astype(BF)
        return carry

    lax.fori_loop(0, FACTOR // 8, narrow, 0, unroll=UNROLL["out"])


def range_forward(pulses, matched_filter, table, twist):
    rows, parts = pulses.shape[1], 8
    filters = matched_filter.reshape(2, FACTOR, FACTOR).transpose(1, 0, 2)
    return pl.pallas_call(
        functools.partial(range_kernel, rows),
        out_shape=jax.ShapeDtypeStruct((FACTOR, 2 * rows, FACTOR), BF),
        in_specs=[HBM] * 4,
        out_specs=VMEM,
        scratch_shapes=[
            pltpu.VMEM((parts, 2, rows, FACTOR * FACTOR // parts), BF),
            pltpu.VMEM((FACTOR, 2, FACTOR), F32),
            pltpu.VMEM((2 * FACTOR, 2 * FACTOR), BF),
            pltpu.VMEM((2, FACTOR, FACTOR), F32),
            pltpu.VMEM((2, FACTOR * (rows + PAD), FACTOR), F32),
            pltpu.VMEM((rows // 2, 2 * FACTOR, 2 * FACTOR), BF),
            pltpu.VMEM((FACTOR * (2 * rows + PAD), FACTOR), F32),
            pltpu.SemaphoreType.DMA((parts + 3,)),
        ],
        compiler_params=pltpu.CompilerParams(vmem_limit_bytes=32 * 2**20),
        cost_estimate=pl.CostEstimate(flops=10**10, bytes_accessed=2**22, transcendentals=0),
        name="range_forward",
    )(*in_hbm(pulses, filters, table, twist))


def image_kernel(rows, tiles, spec_ref, mix_ref, table_ref, twist_ref, last_ref, keep_ref, give_ref, mixed_ref):
    wide = 2 * CHUNK
    for t in range(tiles):
        mix = mix_ref[t].astype(F32)
        mix = jnp.concatenate([mix[:, :wide], mix[:, wide:]], axis=0).T.astype(BF)
        for k2 in range(t * (FACTOR // tiles), (t + 1) * (FACTOR // tiles)):
            mixed_ref[pl.ds(k2 * (wide + PAD), wide), :] = jnp.dot(mix, spec_ref[k2], preferred_element_type=F32)
    pair = 2
    half = last_ref.shape[0] // 2
    core = lax.rem(lax.axis_index("pul"), 2)
    last = jnp.concatenate(
        [
            last_ref[pl.ds(pl.multiple_of(core * half, half), half), :],
            last_ref[pl.ds(pl.multiple_of((1 - core) * half, half), half), :],
        ],
        axis=0,
    )

    def step(s, carry):
        sides = [
            jnp.concatenate(
                [
                    mixed_ref[pl.ds(c * CHUNK + s * pair + j, FACTOR, stride=wide + PAD), :].astype(BF)
                    for c in range(2)
                ],
                axis=0,
            )
            for j in range(pair)
        ]
        wave = jnp.dot(table_ref[...], jnp.concatenate(sides, axis=1), preferred_element_type=F32)
        turned = jnp.concatenate([turn_by(wave, j, twist_ref) for j in range(pair)], axis=0)
        window = times_transposed(last, turned) * (1.0 / FACTOR)
        for j in range(pair):
            keep_ref[s * pair + j] = window[:half, j * FACTOR : (j + 1) * FACTOR].astype(BF)
            give_ref[s * pair + j] = window[half:, j * FACTOR : (j + 1) * FACTOR].astype(BF)
        return carry

    lax.fori_loop(0, CHUNK // pair, step, 0, unroll=UNROLL["image"])


def image_part(spec, mix, table, twist, last):
    tiles, rows = mix.shape[0], mix.shape[1]
    chunks = mix.shape[2] // (4 * CHUNK)
    whole = lambda array: pl.BlockSpec(array.shape, lambda c: (0,) * array.ndim)
    high = last.shape[0]
    return pl.pallas_call(
        functools.partial(image_kernel, rows, tiles),
        grid=(chunks,),
        out_shape=[jax.ShapeDtypeStruct((chunks * CHUNK, high // 2, FACTOR), BF)] * 2,
        in_specs=[
            whole(spec),
            pl.BlockSpec((tiles, rows, 4 * CHUNK), lambda c: (0, 0, c)),
            whole(table),
            whole(twist),
            whole(last),
        ],
        out_specs=[pl.BlockSpec((CHUNK, high // 2, FACTOR), lambda c: (c, 0, 0))] * 2,
        scratch_shapes=[pltpu.VMEM((FACTOR * (2 * CHUNK + PAD), FACTOR), F32)],
        compiler_params=pltpu.CompilerParams(vmem_limit_bytes=32 * 2**20),
        name="image_part",
    )(spec, mix, table, twist, last)


def local(pulses, matched_filter, interp_weights, offsets):
    pul_count, ang_count = lax.axis_size("pul"), lax.axis_size("ang")
    image_rows, rows = pul_count * ang_count, pulses.shape[1]
    azimuth, turn = azimuth_tables(image_rows, rows * pul_count, ang_count)
    mix = mixing(offsets, interp_weights, azimuth, turn)
    mix = lax.all_to_all(
        mix.reshape(pul_count, rows, mix.shape[1]), "pul", split_axis=0, concat_axis=0, tiled=True
    )
    spec = range_forward(pulses, matched_filter, *range_tables())
    keep, give = image_part(spec, mix, *image_tables())
    got = lax.ppermute(give, "pul", [(i, i ^ 1) for i in range(pul_count)])
    part = (keep.astype(F32) + got.astype(F32)).astype(BF)
    parts = lax.all_to_all(part, ("ang", "pul"), split_axis=0, concat_axis=0, tiled=True)
    image = jnp.sum(parts.reshape(image_rows // 2, -1, FACTOR).astype(F32), axis=0)
    return image.reshape(-1, 2, FACTOR).transpose(1, 0, 2).reshape(1, 2, IMAGE_COLS)


def solution(mesh):
    placed = (
        P(None, ("ang", "pul"), None),
        P(),
        P("ang", "pul", None, None),
        P("ang", "pul", None),
    )
    return jax.shard_map(
        local, mesh=mesh, in_specs=placed, out_specs=P(("ang", "pul"), None, None), check_vma=False
    )
```

```python
import functools
import math

import jax
import jax.numpy as jnp
import ml_dtypes
import numpy as np
from jax import lax
from jax.experimental import pallas as pl
from jax.experimental.pallas import tpu as pltpu
from jax.sharding import PartitionSpec as P

FACTOR = 128
BLOCK_ROWS = 32
BAND_PULSES = 64
IMAGE_COLS = 2048
CHUNK = 32

BF = jnp.bfloat16
F32 = jnp.float32


def rounded(values):
    return np.asarray(values, np.float32).astype(ml_dtypes.bfloat16)


def turns(top, bottom):
    angle = np.mod(top, bottom) * (2.0 * math.pi / bottom)
    return np.cos(angle), np.sin(angle)


def complex_matrix(cos, sin):
    return np.block([[cos, -sin], [sin, cos]])


def range_tables():
    at = np.arange(FACTOR)
    grid = at[:, None] * at[None, :]
    cos, sin = turns(-grid, FACTOR)
    table = rounded(complex_matrix(cos, sin))
    twist = np.stack(turns(-grid, FACTOR * FACTOR)).astype(np.float32)
    return table, twist


def image_tables():
    at = np.arange(FACTOR)
    grid = at[:, None] * at[None, :]
    cos, sin = turns(grid, FACTOR)
    table = rounded(complex_matrix(cos, sin))
    twist = np.stack(turns(grid, FACTOR * FACTOR)).astype(np.float32)
    count = IMAGE_COLS // FACTOR
    high = np.arange(count) + (FACTOR * FACTOR - IMAGE_COLS) // 2 // FACTOR
    cos, sin = turns(high[:, None] * at[None, :], FACTOR)
    both = complex_matrix(cos, sin).reshape(2, count, 2 * FACTOR)
    last = rounded(both.transpose(1, 0, 2).reshape(2 * count, 2 * FACTOR))
    return table, twist, last


def azimuth_tables(image_rows, group_pulses, groups):
    total = group_pulses * groups
    chunks = image_rows // CHUNK
    row = np.arange(image_rows) - image_rows // 2
    cos, sin = turns(np.arange(group_pulses)[:, None] * row[None, :], total)
    cos = rounded(cos / math.sqrt(total)).astype(np.float32).reshape(-1, chunks, CHUNK)
    sin = rounded(sin / math.sqrt(total)).astype(np.float32).reshape(-1, chunks, CHUNK)
    table = np.concatenate([cos, sin, -sin, cos], axis=2)
    turn_cos, turn_sin = turns(np.arange(groups)[:, None] * group_pulses * row[None, :], total)
    turn = np.stack([turn_cos, turn_sin], axis=1).reshape(groups, 2, chunks, CHUNK)
    turn = np.where(np.abs(turn) < 1e-9, 0.0, turn)
    turn = np.tile(turn, (1, 1, 1, 4))
    turn[:, 1, :, 2 * CHUNK :] *= -1.0
    turn = turn.transpose(0, 2, 1, 3)
    return rounded(table.reshape(group_pulses, chunks * 4 * CHUNK)), turn.astype(np.float32)


HBM = pl.BlockSpec(memory_space=pltpu.HBM)
VMEM = pl.BlockSpec(memory_space=pltpu.VMEM)
PAD = 1
UNROLL = dict(range=16, out=2, image=16)


def in_hbm(*arrays):
    return [pltpu.with_memory_space_constraint(jnp.asarray(a), pltpu.HBM) for a in arrays]


def fetch(pairs, sems):
    copies = [pltpu.make_async_copy(a, b, sems.at[n]) for n, (a, b) in enumerate(pairs)]
    for copy in copies:
        copy.start()
    return copies


def mixing_kernel(
    blocks, chunks, offsets_hbm, weights_hbm, table_hbm, turn_hbm, out_ref,
    offsets_ref, weights_ref, table_ref, turn_ref, product_ref, total_ref, sems,
):
    width = 4 * CHUNK
    copies = fetch(
        [
            (weights_hbm.at[0, 0], weights_ref),
            (table_hbm, table_ref),
            (offsets_hbm, offsets_ref),
            (turn_hbm.at[lax.axis_index("ang")], turn_ref),
        ],
        sems,
    )
    for copy in copies:
        copy.wait()
    weights = weights_ref[...]
    column = lax.broadcasted_iota(jnp.int32, weights.shape, 1) // BLOCK_ROWS

    def make(chunk):
        columns = pl.ds(pl.multiple_of(chunk * width, width), width)
        total_ref[...] = jnp.zeros_like(total_ref)
        table = table_ref[:, columns]

        def multiply(block, carry):
            own = jnp.where(column == block, weights.astype(F32), 0.0).astype(BF)
            product_ref[block] = jnp.dot(own, table, preferred_element_type=F32)
            return carry

        lax.fori_loop(0, blocks, multiply, 0, unroll=blocks <= 8)

        def place(block, carry):
            window = pl.ds(offsets_ref[0, 0, block], BAND_PULSES)
            total_ref[window, :] += product_ref[block]
            return carry

        lax.fori_loop(0, blocks, place, 0)
        turn = turn_ref[chunk]
        total = total_ref[...]
        other = pltpu.roll(total, width // 2, 1)
        out_ref[:, columns] = (total * turn[0:1] + other * turn[1:2]).astype(BF)

    if chunks == 1:
        make(0)
    else:
        pl.loop(0, chunks)(make)


def mixing(offsets, weights, table, turn):
    group_pulses, width = weights.shape[3], 4 * CHUNK
    chunks, blocks = table.shape[1] // width, offsets.shape[2]
    return pl.pallas_call(
        functools.partial(mixing_kernel, blocks, chunks),
        out_shape=jax.ShapeDtypeStruct((group_pulses, chunks * width), BF),
        in_specs=[HBM] * 4,
        out_specs=VMEM,
        scratch_shapes=[
            pltpu.SMEM(offsets.shape, jnp.int32),
            pltpu.VMEM(weights.shape[2:], BF),
            pltpu.VMEM(table.shape, BF),
            pltpu.VMEM(turn.shape[1:], F32),
            pltpu.VMEM((blocks, BAND_PULSES, width), F32),
            pltpu.VMEM((group_pulses, width), F32),
            pltpu.SemaphoreType.DMA((4,)),
        ],
        compiler_params=pltpu.CompilerParams(vmem_limit_bytes=24 * 2**20),
        name="mixing",
    )(*in_hbm(offsets, weights, table, turn))


def turn_by(wave, j, twist_ref):
    real = wave[:FACTOR, j * FACTOR : (j + 1) * FACTOR]
    imag = wave[FACTOR:, j * FACTOR : (j + 1) * FACTOR]
    cos, sin = twist_ref[0], twist_ref[1]
    return jnp.concatenate([(real * cos - imag * sin).astype(BF), (real * sin + imag * cos).astype(BF)], axis=1)


def times_transposed(left, right):
    return lax.dot_general(left, right, (((1,), (1,)), ((), ())), preferred_element_type=F32)


def range_kernel(
    rows, pulses_hbm, filter_hbm, table_hbm, twist_hbm, out_ref,
    pulses_ref, filter_ref, table_ref, twist_ref, wide_ref, spec_ref, sems,
):
    parts = 8
    length = FACTOR // parts
    pieces = [
        (pulses_hbm.at[:, :, pl.ds(h * length * FACTOR, length * FACTOR)], pulses_ref.at[h]) for h in range(parts)
    ]
    copies = fetch(
        pieces + [(table_hbm, table_ref), (twist_hbm, twist_ref), (filter_hbm, filter_ref)], sems
    )
    for h in range(parts):
        copies[h].wait()
        for m in range(length):
            for c in range(2):
                wide_ref[c, pl.ds((h * length + m) * (rows + PAD), rows), :] = pulses_ref[
                    h, c, :, m * FACTOR : (m + 1) * FACTOR
                ].astype(F32)
    copies[parts].wait()
    copies[parts + 1].wait()
    pair = 2

    copies[parts + 2].wait()
    filter_real = filter_ref[:, 0, :] * (1.0 / FACTOR)
    filter_imag = filter_ref[:, 1, :] * (1.0 / FACTOR)

    def both(s, carry):
        sides = [
            jnp.concatenate(
                [wide_ref[c, pl.ds(s * pair + j, FACTOR, stride=rows + PAD), :].astype(BF) for c in range(2)], axis=0
            )
            for j in range(pair)
        ]
        section = jnp.dot(table_ref[...], jnp.concatenate(sides, axis=1), preferred_element_type=F32)
        turned = jnp.concatenate([turn_by(section, j, twist_ref) for j in range(pair)], axis=0)
        wave = times_transposed(table_ref[...], turned)
        for j in range(pair):
            p = s * pair + j
            real = wave[:FACTOR, j * FACTOR : (j + 1) * FACTOR]
            imag = wave[FACTOR:, j * FACTOR : (j + 1) * FACTOR]
            spec_ref[pl.ds(p, FACTOR, stride=2 * rows + PAD), :] = real * filter_real - imag * filter_imag
            spec_ref[pl.ds(rows + p, FACTOR, stride=2 * rows + PAD), :] = real * filter_imag + imag * filter_real
        return carry

    lax.fori_loop(0, rows // pair, both, 0, unroll=UNROLL["range"])

    def narrow(step, carry):
        begin = pl.multiple_of(step * 8 * (2 * rows + PAD), 8)
        for n in range(8):
            out_ref[step * 8 + n] = spec_ref[pl.ds(begin + n * (2 * rows + PAD), 2 * rows), :].astype(BF)
        return carry

    lax.fori_loop(0, FACTOR // 8, narrow, 0, unroll=UNROLL["out"])


def range_forward(pulses, matched_filter, table, twist):
    rows, parts = pulses.shape[1], 8
    filters = matched_filter.reshape(2, FACTOR, FACTOR).transpose(1, 0, 2)
    return pl.pallas_call(
        functools.partial(range_kernel, rows),
        out_shape=jax.ShapeDtypeStruct((FACTOR, 2 * rows, FACTOR), BF),
        in_specs=[HBM] * 4,
        out_specs=VMEM,
        scratch_shapes=[
            pltpu.VMEM((parts, 2, rows, FACTOR * FACTOR // parts), BF),
            pltpu.VMEM((FACTOR, 2, FACTOR), F32),
            pltpu.VMEM((2 * FACTOR, 2 * FACTOR), BF),
            pltpu.VMEM((2, FACTOR, FACTOR), F32),
            pltpu.VMEM((2, FACTOR * (rows + PAD), FACTOR), F32),
            pltpu.VMEM((FACTOR * (2 * rows + PAD), FACTOR), F32),
            pltpu.SemaphoreType.DMA((parts + 3,)),
        ],
        compiler_params=pltpu.CompilerParams(vmem_limit_bytes=32 * 2**20),
        cost_estimate=pl.CostEstimate(flops=10**10, bytes_accessed=2**22, transcendentals=0),
        name="range_forward",
    )(*in_hbm(pulses, filters, table, twist))


def image_kernel(rows, tiles, spec_ref, mix_ref, table_ref, twist_ref, last_ref, keep_ref, give_ref, mixed_ref):
    wide = 2 * CHUNK
    for t in range(tiles):
        mix = mix_ref[t].astype(F32)
        mix = jnp.concatenate([mix[:, :wide], mix[:, wide:]], axis=0).T.astype(BF)
        for k2 in range(t * (FACTOR // tiles), (t + 1) * (FACTOR // tiles)):
            mixed_ref[pl.ds(k2 * (wide + PAD), wide), :] = jnp.dot(mix, spec_ref[k2], preferred_element_type=F32)
    pair = 2
    half = last_ref.shape[0] // 2
    core = lax.rem(lax.axis_index("pul"), 2)
    last = jnp.concatenate(
        [
            last_ref[pl.ds(pl.multiple_of(core * half, half), half), :],
            last_ref[pl.ds(pl.multiple_of((1 - core) * half, half), half), :],
        ],
        axis=0,
    )

    def step(s, carry):
        sides = [
            jnp.concatenate(
                [
                    mixed_ref[pl.ds(c * CHUNK + s * pair + j, FACTOR, stride=wide + PAD), :].astype(BF)
                    for c in range(2)
                ],
                axis=0,
            )
            for j in range(pair)
        ]
        wave = jnp.dot(table_ref[...], jnp.concatenate(sides, axis=1), preferred_element_type=F32)
        turned = jnp.concatenate([turn_by(wave, j, twist_ref) for j in range(pair)], axis=0)
        window = times_transposed(last, turned) * (1.0 / FACTOR)
        for j in range(pair):
            keep_ref[s * pair + j] = window[:half, j * FACTOR : (j + 1) * FACTOR].astype(BF)
            give_ref[s * pair + j] = window[half:, j * FACTOR : (j + 1) * FACTOR].astype(BF)
        return carry

    lax.fori_loop(0, CHUNK // pair, step, 0, unroll=UNROLL["image"])


def image_part(spec, mix, table, twist, last):
    tiles, rows = mix.shape[0], mix.shape[1]
    chunks = mix.shape[2] // (4 * CHUNK)
    whole = lambda array: pl.BlockSpec(array.shape, lambda c: (0,) * array.ndim)
    high = last.shape[0]
    return pl.pallas_call(
        functools.partial(image_kernel, rows, tiles),
        grid=(chunks,),
        out_shape=[jax.ShapeDtypeStruct((chunks * CHUNK, high // 2, FACTOR), BF)] * 2,
        in_specs=[
            whole(spec),
            pl.BlockSpec((tiles, rows, 4 * CHUNK), lambda c: (0, 0, c)),
            whole(table),
            whole(twist),
            whole(last),
        ],
        out_specs=[pl.BlockSpec((CHUNK, high // 2, FACTOR), lambda c: (c, 0, 0))] * 2,
        scratch_shapes=[pltpu.VMEM((FACTOR * (2 * CHUNK + PAD), FACTOR), F32)],
        compiler_params=pltpu.CompilerParams(vmem_limit_bytes=32 * 2**20),
        name="image_part",
    )(spec, mix, table, twist, last)


def local(pulses, matched_filter, interp_weights, offsets):
    pul_count, ang_count = lax.axis_size("pul"), lax.axis_size("ang")
    image_rows, rows = pul_count * ang_count, pulses.shape[1]
    azimuth, turn = azimuth_tables(image_rows, rows * pul_count, ang_count)
    mix = mixing(offsets, interp_weights, azimuth, turn)
    mix = lax.all_to_all(
        mix.reshape(pul_count, rows, mix.shape[1]), "pul", split_axis=0, concat_axis=0, tiled=True
    )
    spec = range_forward(pulses, matched_filter, *range_tables())
    keep, give = image_part(spec, mix, *image_tables())
    got = lax.ppermute(give, "pul", [(i, i ^ 1) for i in range(pul_count)])
    part = (keep.astype(F32) + got.astype(F32)).astype(BF)
    parts = lax.all_to_all(part, ("ang", "pul"), split_axis=0, concat_axis=0, tiled=True)
    image = jnp.sum(parts.reshape(image_rows // 2, -1, FACTOR).astype(F32), axis=0)
    return image.reshape(-1, 2, FACTOR).transpose(1, 0, 2).reshape(1, 2, IMAGE_COLS)


def solution(mesh):
    placed = (
        P(None, ("ang", "pul"), None),
        P(),
        P("ang", "pul", None, None),
        P("ang", "pul", None),
    )
    return jax.shard_map(
        local, mesh=mesh, in_specs=placed, out_specs=P(("ang", "pul"), None, None), check_vma=False
    )
```

```python
import functools
import math

import jax
import jax.numpy as jnp
import ml_dtypes
import numpy as np
from jax import lax
from jax.experimental import pallas as pl
from jax.experimental.pallas import tpu as pltpu
from jax.sharding import PartitionSpec as P

FACTOR = 128
BLOCK_ROWS = 32
BAND_PULSES = 64
IMAGE_COLS = 2048
CHUNK = 32

BF = jnp.bfloat16
F32 = jnp.float32


def rounded(values):
    return np.asarray(values, np.float32).astype(ml_dtypes.bfloat16)


def turns(top, bottom):
    angle = np.mod(top, bottom) * (2.0 * math.pi / bottom)
    return np.cos(angle), np.sin(angle)


def complex_matrix(cos, sin):
    return np.block([[cos, -sin], [sin, cos]])


def range_tables():
    at = np.arange(FACTOR)
    grid = at[:, None] * at[None, :]
    cos, sin = turns(-grid, FACTOR)
    table = rounded(complex_matrix(cos, sin))
    twist = np.stack(turns(-grid, FACTOR * FACTOR)).astype(np.float32)
    return table, twist


def image_tables():
    at = np.arange(FACTOR)
    grid = at[:, None] * at[None, :]
    cos, sin = turns(grid, FACTOR)
    table = rounded(complex_matrix(cos, sin))
    twist = np.stack(turns(grid, FACTOR * FACTOR)).astype(np.float32)
    count = IMAGE_COLS // FACTOR
    high = np.arange(count) + (FACTOR * FACTOR - IMAGE_COLS) // 2 // FACTOR
    cos, sin = turns(high[:, None] * at[None, :], FACTOR)
    both = complex_matrix(cos, sin).reshape(2, count, 2 * FACTOR)
    last = rounded(both.transpose(1, 0, 2).reshape(2 * count, 2 * FACTOR))
    return table, twist, last


def azimuth_tables(image_rows, group_pulses, groups):
    total = group_pulses * groups
    chunks = image_rows // CHUNK
    row = np.arange(image_rows) - image_rows // 2
    cos, sin = turns(np.arange(group_pulses)[:, None] * row[None, :], total)
    cos = rounded(cos / math.sqrt(total)).astype(np.float32).reshape(-1, chunks, CHUNK)
    sin = rounded(sin / math.sqrt(total)).astype(np.float32).reshape(-1, chunks, CHUNK)
    table = np.concatenate([cos, sin, -sin, cos], axis=2)
    turn_cos, turn_sin = turns(np.arange(groups)[:, None] * group_pulses * row[None, :], total)
    turn = np.stack([turn_cos, turn_sin], axis=1).reshape(groups, 2, chunks, CHUNK)
    turn = np.where(np.abs(turn) < 1e-9, 0.0, turn)
    turn = np.tile(turn, (1, 1, 1, 4))
    turn[:, 1, :, 2 * CHUNK :] *= -1.0
    turn = turn.transpose(0, 2, 1, 3)
    return rounded(table.reshape(group_pulses, chunks * 4 * CHUNK)), turn.astype(np.float32)


HBM = pl.BlockSpec(memory_space=pltpu.HBM)
VMEM = pl.BlockSpec(memory_space=pltpu.VMEM)
PAD = 1
UNROLL = dict(range=16, out=2, image=16)


def in_hbm(*arrays):
    return [pltpu.with_memory_space_constraint(jnp.asarray(a), pltpu.HBM) for a in arrays]


def fetch(pairs, sems):
    copies = [pltpu.make_async_copy(a, b, sems.at[n]) for n, (a, b) in enumerate(pairs)]
    for copy in copies:
        copy.start()
    return copies


def mixing_kernel(
    blocks, chunks, offsets_hbm, weights_hbm, table_hbm, turn_hbm, pulses_hbm, out_ref, real_ref,
    offsets_ref, weights_ref, table_ref, turn_ref, product_ref, total_ref, sems,
):
    width = 4 * CHUNK
    copies = fetch(
        [
            (weights_hbm.at[0, 0], weights_ref),
            (table_hbm, table_ref),
            (offsets_hbm, offsets_ref),
            (turn_hbm.at[lax.axis_index("ang")], turn_ref),
            (pulses_hbm.at[0], real_ref),
        ],
        sems,
    )
    for copy in copies[:4]:
        copy.wait()
    weights = weights_ref[...]
    column = lax.broadcasted_iota(jnp.int32, weights.shape, 1) // BLOCK_ROWS

    def make(chunk):
        columns = pl.ds(pl.multiple_of(chunk * width, width), width)
        total_ref[...] = jnp.zeros_like(total_ref)
        table = table_ref[:, columns]

        def multiply(block, carry):
            own = jnp.where(column == block, weights.astype(F32), 0.0).astype(BF)
            product_ref[block] = jnp.dot(own, table, preferred_element_type=F32)
            return carry

        lax.fori_loop(0, blocks, multiply, 0, unroll=blocks <= 8)

        def place(block, carry):
            window = pl.ds(offsets_ref[0, 0, block], BAND_PULSES)
            total_ref[window, :] += product_ref[block]
            return carry

        lax.fori_loop(0, blocks, place, 0)
        turn = turn_ref[chunk]
        total = total_ref[...]
        other = pltpu.roll(total, width // 2, 1)
        out_ref[:, columns] = (total * turn[0:1] + other * turn[1:2]).astype(BF)

    if chunks == 1:
        make(0)
    else:
        pl.loop(0, chunks)(make)
    copies[4].wait()


def mixing(offsets, weights, table, turn, pulses):
    group_pulses, width = weights.shape[3], 4 * CHUNK
    chunks, blocks = table.shape[1] // width, offsets.shape[2]
    return pl.pallas_call(
        functools.partial(mixing_kernel, blocks, chunks),
        out_shape=[
            jax.ShapeDtypeStruct((group_pulses, chunks * width), BF),
            jax.ShapeDtypeStruct(pulses.shape[1:], BF),
        ],
        in_specs=[HBM] * 5,
        out_specs=[VMEM, VMEM],
        scratch_shapes=[
            pltpu.SMEM(offsets.shape, jnp.int32),
            pltpu.VMEM(weights.shape[2:], BF),
            pltpu.VMEM(table.shape, BF),
            pltpu.VMEM(turn.shape[1:], F32),
            pltpu.VMEM((blocks, BAND_PULSES, width), F32),
            pltpu.VMEM((group_pulses, width), F32),
            pltpu.SemaphoreType.DMA((5,)),
        ],
        compiler_params=pltpu.CompilerParams(vmem_limit_bytes=24 * 2**20),
        name="mixing",
    )(*in_hbm(offsets, weights, table, turn, pulses))


def turn_by(wave, j, twist_ref):
    real = wave[:FACTOR, j * FACTOR : (j + 1) * FACTOR]
    imag = wave[FACTOR:, j * FACTOR : (j + 1) * FACTOR]
    cos, sin = twist_ref[0], twist_ref[1]
    return jnp.concatenate([(real * cos - imag * sin).astype(BF), (real * sin + imag * cos).astype(BF)], axis=1)


def times_transposed(left, right):
    return lax.dot_general(left, right, (((1,), (1,)), ((), ())), preferred_element_type=F32)


def range_kernel(
    rows, real_ref, pulses_hbm, filter_hbm, table_hbm, twist_hbm, out_ref,
    imag_ref, filter_ref, table_ref, twist_ref, wide_ref, spec_ref, sems,
):
    parts = 4
    length = FACTOR // parts
    pieces = [
        (pulses_hbm.at[1, :, pl.ds(h * length * FACTOR, length * FACTOR)], imag_ref.at[h]) for h in range(parts)
    ]
    copies = fetch(
        pieces + [(table_hbm, table_ref), (twist_hbm, twist_ref), (filter_hbm, filter_ref)], sems
    )
    for m in range(FACTOR):
        wide_ref[0, pl.ds(m * (rows + PAD), rows), :] = real_ref[:, m * FACTOR : (m + 1) * FACTOR].astype(F32)
    for h in range(parts):
        copies[h].wait()
        for m in range(length):
            wide_ref[1, pl.ds((h * length + m) * (rows + PAD), rows), :] = imag_ref[
                h, :, m * FACTOR : (m + 1) * FACTOR
            ].astype(F32)
    copies[parts].wait()
    copies[parts + 1].wait()
    pair = 2

    copies[parts + 2].wait()
    filter_real = filter_ref[:, 0, :] * (1.0 / FACTOR)
    filter_imag = filter_ref[:, 1, :] * (1.0 / FACTOR)

    def both(s, carry):
        sides = [
            jnp.concatenate(
                [wide_ref[c, pl.ds(s * pair + j, FACTOR, stride=rows + PAD), :].astype(BF) for c in range(2)], axis=0
            )
            for j in range(pair)
        ]
        section = jnp.dot(table_ref[...], jnp.concatenate(sides, axis=1), preferred_element_type=F32)
        turned = jnp.concatenate([turn_by(section, j, twist_ref) for j in range(pair)], axis=0)
        wave = times_transposed(table_ref[...], turned)
        for j in range(pair):
            p = s * pair + j
            real = wave[:FACTOR, j * FACTOR : (j + 1) * FACTOR]
            imag = wave[FACTOR:, j * FACTOR : (j + 1) * FACTOR]
            spec_ref[pl.ds(p, FACTOR, stride=2 * rows + PAD), :] = real * filter_real - imag * filter_imag
            spec_ref[pl.ds(rows + p, FACTOR, stride=2 * rows + PAD), :] = real * filter_imag + imag * filter_real
        return carry

    lax.fori_loop(0, rows // pair, both, 0, unroll=UNROLL["range"])

    def narrow(step, carry):
        begin = pl.multiple_of(step * 8 * (2 * rows + PAD), 8)
        for n in range(8):
            out_ref[step * 8 + n] = spec_ref[pl.ds(begin + n * (2 * rows + PAD), 2 * rows), :].astype(BF)
        return carry

    lax.fori_loop(0, FACTOR // 8, narrow, 0, unroll=UNROLL["out"])


def range_forward(real, pulses, matched_filter, table, twist):
    rows, parts = pulses.shape[1], 4
    filters = matched_filter.reshape(2, FACTOR, FACTOR).transpose(1, 0, 2)
    return pl.pallas_call(
        functools.partial(range_kernel, rows),
        out_shape=jax.ShapeDtypeStruct((FACTOR, 2 * rows, FACTOR), BF),
        in_specs=[VMEM] + [HBM] * 4,
        out_specs=VMEM,
        scratch_shapes=[
            pltpu.VMEM((parts, rows, FACTOR * FACTOR // parts), BF),
            pltpu.VMEM((FACTOR, 2, FACTOR), F32),
            pltpu.VMEM((2 * FACTOR, 2 * FACTOR), BF),
            pltpu.VMEM((2, FACTOR, FACTOR), F32),
            pltpu.VMEM((2, FACTOR * (rows + PAD), FACTOR), F32),
            pltpu.VMEM((FACTOR * (2 * rows + PAD), FACTOR), F32),
            pltpu.SemaphoreType.DMA((parts + 3,)),
        ],
        compiler_params=pltpu.CompilerParams(vmem_limit_bytes=32 * 2**20),
        cost_estimate=pl.CostEstimate(flops=10**10, bytes_accessed=2**22, transcendentals=0),
        name="range_forward",
    )(real, *in_hbm(pulses, filters, table, twist))


def image_kernel(rows, tiles, spec_ref, mix_ref, table_ref, twist_ref, last_ref, keep_ref, give_ref, mixed_ref):
    wide = 2 * CHUNK
    for t in range(tiles):
        mix = mix_ref[t].astype(F32)
        mix = jnp.concatenate([mix[:, :wide], mix[:, wide:]], axis=0).T.astype(BF)
        for k2 in range(t * (FACTOR // tiles), (t + 1) * (FACTOR // tiles)):
            mixed_ref[pl.ds(k2 * (wide + PAD), wide), :] = jnp.dot(mix, spec_ref[k2], preferred_element_type=F32)
    pair = 2
    half = last_ref.shape[0] // 2
    core = lax.rem(lax.axis_index("pul"), 2)
    last = jnp.concatenate(
        [
            last_ref[pl.ds(pl.multiple_of(core * half, half), half), :],
            last_ref[pl.ds(pl.multiple_of((1 - core) * half, half), half), :],
        ],
        axis=0,
    )

    def step(s, carry):
        sides = [
            jnp.concatenate(
                [
                    mixed_ref[pl.ds(c * CHUNK + s * pair + j, FACTOR, stride=wide + PAD), :].astype(BF)
                    for c in range(2)
                ],
                axis=0,
            )
            for j in range(pair)
        ]
        wave = jnp.dot(table_ref[...], jnp.concatenate(sides, axis=1), preferred_element_type=F32)
        turned = jnp.concatenate([turn_by(wave, j, twist_ref) for j in range(pair)], axis=0)
        window = times_transposed(last, turned) * (1.0 / FACTOR)
        for j in range(pair):
            keep_ref[s * pair + j] = window[:half, j * FACTOR : (j + 1) * FACTOR].astype(BF)
            give_ref[s * pair + j] = window[half:, j * FACTOR : (j + 1) * FACTOR].astype(BF)
        return carry

    lax.fori_loop(0, CHUNK // pair, step, 0, unroll=UNROLL["image"])


def image_part(spec, mix, table, twist, last):
    tiles, rows = mix.shape[0], mix.shape[1]
    chunks = mix.shape[2] // (4 * CHUNK)
    whole = lambda array: pl.BlockSpec(array.shape, lambda c: (0,) * array.ndim)
    high = last.shape[0]
    return pl.pallas_call(
        functools.partial(image_kernel, rows, tiles),
        grid=(chunks,),
        out_shape=[jax.ShapeDtypeStruct((chunks * CHUNK, high // 2, FACTOR), BF)] * 2,
        in_specs=[
            whole(spec),
            pl.BlockSpec((tiles, rows, 4 * CHUNK), lambda c: (0, 0, c)),
            whole(table),
            whole(twist),
            whole(last),
        ],
        out_specs=[pl.BlockSpec((CHUNK, high // 2, FACTOR), lambda c: (c, 0, 0))] * 2,
        scratch_shapes=[pltpu.VMEM((FACTOR * (2 * CHUNK + PAD), FACTOR), F32)],
        compiler_params=pltpu.CompilerParams(vmem_limit_bytes=32 * 2**20),
        name="image_part",
    )(spec, mix, table, twist, last)


def local(pulses, matched_filter, interp_weights, offsets):
    pul_count, ang_count = lax.axis_size("pul"), lax.axis_size("ang")
    image_rows, rows = pul_count * ang_count, pulses.shape[1]
    azimuth, turn = azimuth_tables(image_rows, rows * pul_count, ang_count)
    mix, real = mixing(offsets, interp_weights, azimuth, turn, pulses)
    mix = lax.all_to_all(
        mix.reshape(pul_count, rows, mix.shape[1]), "pul", split_axis=0, concat_axis=0, tiled=True
    )
    spec = range_forward(real, pulses, matched_filter, *range_tables())
    keep, give = image_part(spec, mix, *image_tables())
    got = lax.ppermute(give, "pul", [(i, i ^ 1) for i in range(pul_count)])
    part = (keep.astype(F32) + got.astype(F32)).astype(BF)
    parts = lax.all_to_all(part, ("ang", "pul"), split_axis=0, concat_axis=0, tiled=True)
    image = jnp.sum(parts.reshape(image_rows // 2, -1, FACTOR).astype(F32), axis=0)
    return image.reshape(-1, 2, FACTOR).transpose(1, 0, 2).reshape(1, 2, IMAGE_COLS)


def solution(mesh):
    placed = (
        P(None, ("ang", "pul"), None),
        P(),
        P("ang", "pul", None, None),
        P("ang", "pul", None),
    )
    return jax.shard_map(
        local, mesh=mesh, in_specs=placed, out_specs=P(("ang", "pul"), None, None), check_vma=False
    )
```

```python
import functools
import math

import jax
import jax.numpy as jnp
import ml_dtypes
import numpy as np
from jax import lax
from jax.experimental import pallas as pl
from jax.experimental.pallas import tpu as pltpu
from jax.sharding import PartitionSpec as P

FACTOR = 128
BLOCK_ROWS = 32
BAND_PULSES = 64
IMAGE_COLS = 2048
CHUNK = 32

BF = jnp.bfloat16
F32 = jnp.float32


def rounded(values):
    return np.asarray(values, np.float32).astype(ml_dtypes.bfloat16)


def turns(top, bottom):
    angle = np.mod(top, bottom) * (2.0 * math.pi / bottom)
    return np.cos(angle), np.sin(angle)


def complex_matrix(cos, sin):
    return np.block([[cos, -sin], [sin, cos]])


def range_tables():
    at = np.arange(FACTOR)
    grid = at[:, None] * at[None, :]
    cos, sin = turns(-grid, FACTOR)
    table = rounded(complex_matrix(cos, sin))
    twist = np.stack(turns(-grid, FACTOR * FACTOR)).astype(np.float32)
    return table, twist


def image_tables():
    at = np.arange(FACTOR)
    grid = at[:, None] * at[None, :]
    cos, sin = turns(grid, FACTOR)
    table = rounded(complex_matrix(cos, sin))
    twist = np.stack(turns(grid, FACTOR * FACTOR)).astype(np.float32)
    count = IMAGE_COLS // FACTOR
    high = np.arange(count) + (FACTOR * FACTOR - IMAGE_COLS) // 2 // FACTOR
    cos, sin = turns(high[:, None] * at[None, :], FACTOR)
    both = complex_matrix(cos, sin).reshape(2, count, 2 * FACTOR)
    last = rounded(both.transpose(1, 0, 2).reshape(2 * count, 2 * FACTOR))
    return table, twist, last


def azimuth_tables(image_rows, group_pulses, groups):
    total = group_pulses * groups
    chunks = image_rows // CHUNK
    row = np.arange(image_rows) - image_rows // 2
    cos, sin = turns(np.arange(group_pulses)[:, None] * row[None, :], total)
    cos = rounded(cos / math.sqrt(total)).astype(np.float32).reshape(-1, chunks, CHUNK)
    sin = rounded(sin / math.sqrt(total)).astype(np.float32).reshape(-1, chunks, CHUNK)
    table = np.concatenate([cos, sin, -sin, cos], axis=2)
    turn_cos, turn_sin = turns(np.arange(groups)[:, None] * group_pulses * row[None, :], total)
    turn = np.stack([turn_cos, turn_sin], axis=1).reshape(groups, 2, chunks, CHUNK)
    turn = np.where(np.abs(turn) < 1e-9, 0.0, turn)
    turn = np.tile(turn, (1, 1, 1, 4))
    turn[:, 1, :, 2 * CHUNK :] *= -1.0
    turn = turn.transpose(0, 2, 1, 3)
    return rounded(table.reshape(group_pulses, chunks * 4 * CHUNK)), turn.astype(np.float32)


HBM = pl.BlockSpec(memory_space=pltpu.HBM)
VMEM = pl.BlockSpec(memory_space=pltpu.VMEM)
PAD = 1
UNROLL = dict(range=16, out=2, image=16)


def in_hbm(*arrays):
    return [pltpu.with_memory_space_constraint(jnp.asarray(a), pltpu.HBM) for a in arrays]


def fetch(pairs, sems):
    copies = [pltpu.make_async_copy(a, b, sems.at[n]) for n, (a, b) in enumerate(pairs)]
    for copy in copies:
        copy.start()
    return copies


def mixing_kernel(
    blocks, chunks, offsets_hbm, weights_hbm, table_hbm, turn_hbm, pulses_hbm, out_ref, real_ref,
    offsets_ref, weights_ref, table_ref, turn_ref, product_ref, total_ref, sems,
):
    width = 4 * CHUNK
    copies = fetch(
        [
            (weights_hbm.at[0, 0], weights_ref),
            (table_hbm, table_ref),
            (offsets_hbm, offsets_ref),
            (turn_hbm.at[lax.axis_index("ang")], turn_ref),
            (pulses_hbm.at[0], real_ref),
        ],
        sems,
    )
    for copy in copies[:4]:
        copy.wait()
    weights = weights_ref[...]
    column = lax.broadcasted_iota(jnp.int32, weights.shape, 1) // BLOCK_ROWS

    def make(chunk):
        columns = pl.ds(pl.multiple_of(chunk * width, width), width)
        total_ref[...] = jnp.zeros_like(total_ref)
        table = table_ref[:, columns]

        def multiply(block, carry):
            own = jnp.where(column == block, weights.astype(F32), 0.0).astype(BF)
            product_ref[block] = jnp.dot(own, table, preferred_element_type=F32)
            return carry

        lax.fori_loop(0, blocks, multiply, 0, unroll=blocks <= 8)

        def place(block, carry):
            window = pl.ds(offsets_ref[0, 0, block], BAND_PULSES)
            total_ref[window, :] += product_ref[block]
            return carry

        lax.fori_loop(0, blocks, place, 0)
        turn = turn_ref[chunk]
        total = total_ref[...]
        other = pltpu.roll(total, width // 2, 1)
        mixed = total * turn[0:1] + other * turn[1:2]
        lower = mixed.reshape(-1, 2, 16, width)[:, 0]
        upper = pltpu.roll(mixed, width // 2, 1).reshape(-1, 2, 16, width)[:, 1]
        lane = lax.broadcasted_iota(jnp.int32, lower.shape, 2)
        out_ref[:, columns] = jnp.where(lane < width // 2, lower, upper).reshape(-1, width).astype(BF)

    if chunks == 1:
        make(0)
    else:
        pl.loop(0, chunks)(make)
    copies[4].wait()


def mixing(offsets, weights, table, turn, pulses):
    group_pulses, width = weights.shape[3], 4 * CHUNK
    chunks, blocks = table.shape[1] // width, offsets.shape[2]
    return pl.pallas_call(
        functools.partial(mixing_kernel, blocks, chunks),
        out_shape=[
            jax.ShapeDtypeStruct((group_pulses // 2, chunks * width), BF),
            jax.ShapeDtypeStruct(pulses.shape[1:], BF),
        ],
        in_specs=[HBM] * 5,
        out_specs=[VMEM, VMEM],
        scratch_shapes=[
            pltpu.SMEM(offsets.shape, jnp.int32),
            pltpu.VMEM(weights.shape[2:], BF),
            pltpu.VMEM(table.shape, BF),
            pltpu.VMEM(turn.shape[1:], F32),
            pltpu.VMEM((blocks, BAND_PULSES, width), F32),
            pltpu.VMEM((group_pulses, width), F32),
            pltpu.SemaphoreType.DMA((5,)),
        ],
        compiler_params=pltpu.CompilerParams(vmem_limit_bytes=24 * 2**20),
        name="mixing",
    )(*in_hbm(offsets, weights, table, turn, pulses))


def turn_by(wave, j, twist_ref):
    real = wave[:FACTOR, j * FACTOR : (j + 1) * FACTOR]
    imag = wave[FACTOR:, j * FACTOR : (j + 1) * FACTOR]
    cos, sin = twist_ref[0], twist_ref[1]
    return jnp.concatenate([(real * cos - imag * sin).astype(BF), (real * sin + imag * cos).astype(BF)], axis=1)


def times_transposed(left, right):
    return lax.dot_general(left, right, (((1,), (1,)), ((), ())), preferred_element_type=F32)


def range_kernel(
    rows, real_ref, pulses_hbm, filter_hbm, table_hbm, twist_hbm, out_ref,
    imag_ref, filter_ref, table_ref, twist_ref, wide_ref, spec_ref, sems,
):
    parts = 4
    length = FACTOR // parts
    pieces = [
        (pulses_hbm.at[1, :, pl.ds(h * length * FACTOR, length * FACTOR)], imag_ref.at[h]) for h in range(parts)
    ]
    copies = fetch(
        pieces + [(table_hbm, table_ref), (twist_hbm, twist_ref), (filter_hbm, filter_ref)], sems
    )
    for m in range(FACTOR):
        wide_ref[0, pl.ds(m * (rows + PAD), rows), :] = real_ref[:, m * FACTOR : (m + 1) * FACTOR].astype(F32)
    for h in range(parts):
        copies[h].wait()
        for m in range(length):
            wide_ref[1, pl.ds((h * length + m) * (rows + PAD), rows), :] = imag_ref[
                h, :, m * FACTOR : (m + 1) * FACTOR
            ].astype(F32)
    copies[parts].wait()
    copies[parts + 1].wait()
    pair = 2

    copies[parts + 2].wait()
    filter_real = filter_ref[:, 0, :] * (1.0 / FACTOR)
    filter_imag = filter_ref[:, 1, :] * (1.0 / FACTOR)

    def both(s, carry):
        sides = [
            jnp.concatenate(
                [wide_ref[c, pl.ds(s * pair + j, FACTOR, stride=rows + PAD), :].astype(BF) for c in range(2)], axis=0
            )
            for j in range(pair)
        ]
        section = jnp.dot(table_ref[...], jnp.concatenate(sides, axis=1), preferred_element_type=F32)
        turned = jnp.concatenate([turn_by(section, j, twist_ref) for j in range(pair)], axis=0)
        wave = times_transposed(table_ref[...], turned)
        for j in range(pair):
            p = s * pair + j
            real = wave[:FACTOR, j * FACTOR : (j + 1) * FACTOR]
            imag = wave[FACTOR:, j * FACTOR : (j + 1) * FACTOR]
            spec_ref[pl.ds(p, FACTOR, stride=2 * rows + PAD), :] = real * filter_real - imag * filter_imag
            spec_ref[pl.ds(rows + p, FACTOR, stride=2 * rows + PAD), :] = real * filter_imag + imag * filter_real
        return carry

    lax.fori_loop(0, rows // pair, both, 0, unroll=UNROLL["range"])

    def narrow(step, carry):
        begin = pl.multiple_of(step * 8 * (2 * rows + PAD), 8)
        for n in range(8):
            out_ref[step * 8 + n] = spec_ref[pl.ds(begin + n * (2 * rows + PAD), 2 * rows), :].astype(BF)
        return carry

    lax.fori_loop(0, FACTOR // 8, narrow, 0, unroll=UNROLL["out"])


def range_forward(real, pulses, matched_filter, table, twist):
    rows, parts = pulses.shape[1], 4
    filters = matched_filter.reshape(2, FACTOR, FACTOR).transpose(1, 0, 2)
    return pl.pallas_call(
        functools.partial(range_kernel, rows),
        out_shape=jax.ShapeDtypeStruct((FACTOR, 2 * rows, FACTOR), BF),
        in_specs=[VMEM] + [HBM] * 4,
        out_specs=VMEM,
        scratch_shapes=[
            pltpu.VMEM((parts, rows, FACTOR * FACTOR // parts), BF),
            pltpu.VMEM((FACTOR, 2, FACTOR), F32),
            pltpu.VMEM((2 * FACTOR, 2 * FACTOR), BF),
            pltpu.VMEM((2, FACTOR, FACTOR), F32),
            pltpu.VMEM((2, FACTOR * (rows + PAD), FACTOR), F32),
            pltpu.VMEM((FACTOR * (2 * rows + PAD), FACTOR), F32),
            pltpu.SemaphoreType.DMA((parts + 3,)),
        ],
        compiler_params=pltpu.CompilerParams(vmem_limit_bytes=32 * 2**20),
        cost_estimate=pl.CostEstimate(flops=10**10, bytes_accessed=2**22, transcendentals=0),
        name="range_forward",
    )(real, *in_hbm(pulses, filters, table, twist))


def image_kernel(rows, tiles, spec_ref, mix_ref, table_ref, twist_ref, last_ref, keep_ref, give_ref, mixed_ref):
    wide = 2 * CHUNK
    for t in range(tiles):
        mix = mix_ref[t].astype(F32)
        mix = jnp.concatenate([mix[:, :wide], mix[:, wide:]], axis=0)
        turned = jnp.concatenate([-mix[:, CHUNK:], mix[:, :CHUNK]], axis=1)
        mix = jnp.concatenate([mix, turned], axis=0).T.astype(BF)
        for k2 in range(t * (FACTOR // tiles), (t + 1) * (FACTOR // tiles)):
            mixed_ref[pl.ds(k2 * (wide + PAD), wide), :] = jnp.dot(mix, spec_ref[k2], preferred_element_type=F32)
    pair = 2
    half = last_ref.shape[0] // 2
    core = lax.rem(lax.axis_index("pul"), 2)
    last = jnp.concatenate(
        [
            last_ref[pl.ds(pl.multiple_of(core * half, half), half), :],
            last_ref[pl.ds(pl.multiple_of((1 - core) * half, half), half), :],
        ],
        axis=0,
    )

    def step(s, carry):
        sides = [
            jnp.concatenate(
                [
                    mixed_ref[pl.ds(c * CHUNK + s * pair + j, FACTOR, stride=wide + PAD), :].astype(BF)
                    for c in range(2)
                ],
                axis=0,
            )
            for j in range(pair)
        ]
        wave = jnp.dot(table_ref[...], jnp.concatenate(sides, axis=1), preferred_element_type=F32)
        turned = jnp.concatenate([turn_by(wave, j, twist_ref) for j in range(pair)], axis=0)
        window = times_transposed(last, turned) * (1.0 / FACTOR)
        for j in range(pair):
            keep_ref[s * pair + j] = window[:half, j * FACTOR : (j + 1) * FACTOR].astype(BF)
            give_ref[s * pair + j] = window[half:, j * FACTOR : (j + 1) * FACTOR].astype(BF)
        return carry

    lax.fori_loop(0, CHUNK // pair, step, 0, unroll=UNROLL["image"])


def image_part(spec, mix, table, twist, last):
    tiles, rows = mix.shape[0], mix.shape[1]
    chunks = mix.shape[2] // (4 * CHUNK)
    whole = lambda array: pl.BlockSpec(array.shape, lambda c: (0,) * array.ndim)
    high = last.shape[0]
    return pl.pallas_call(
        functools.partial(image_kernel, rows, tiles),
        grid=(chunks,),
        out_shape=[jax.ShapeDtypeStruct((chunks * CHUNK, high // 2, FACTOR), BF)] * 2,
        in_specs=[
            whole(spec),
            pl.BlockSpec((tiles, rows, 4 * CHUNK), lambda c: (0, 0, c)),
            whole(table),
            whole(twist),
            whole(last),
        ],
        out_specs=[pl.BlockSpec((CHUNK, high // 2, FACTOR), lambda c: (c, 0, 0))] * 2,
        scratch_shapes=[pltpu.VMEM((FACTOR * (2 * CHUNK + PAD), FACTOR), F32)],
        compiler_params=pltpu.CompilerParams(vmem_limit_bytes=32 * 2**20),
        name="image_part",
    )(spec, mix, table, twist, last)


def local(pulses, matched_filter, interp_weights, offsets):
    pul_count, ang_count = lax.axis_size("pul"), lax.axis_size("ang")
    image_rows, rows = pul_count * ang_count, pulses.shape[1]
    azimuth, turn = azimuth_tables(image_rows, rows * pul_count, ang_count)
    mix, real = mixing(offsets, interp_weights, azimuth, turn, pulses)
    mix = lax.all_to_all(
        mix.reshape(pul_count, rows // 2, mix.shape[1]), "pul", split_axis=0, concat_axis=0, tiled=True
    )
    spec = range_forward(real, pulses, matched_filter, *range_tables())
    keep, give = image_part(spec, mix, *image_tables())
    got = lax.ppermute(give, "pul", [(i, i ^ 1) for i in range(pul_count)])
    part = (keep.astype(F32) + got.astype(F32)).astype(BF)
    parts = lax.all_to_all(part, ("ang", "pul"), split_axis=0, concat_axis=0, tiled=True)
    image = jnp.sum(parts.reshape(image_rows // 2, -1, FACTOR).astype(F32), axis=0)
    return image.reshape(-1, 2, FACTOR).transpose(1, 0, 2).reshape(1, 2, IMAGE_COLS)


def solution(mesh):
    placed = (
        P(None, ("ang", "pul"), None),
        P(),
        P("ang", "pul", None, None),
        P("ang", "pul", None),
    )
    return jax.shard_map(
        local, mesh=mesh, in_specs=placed, out_specs=P(("ang", "pul"), None, None), check_vma=False
    )
```
